1024 devices in a mesh: group: 16 (over y, x), cuts: 64 (over z, core).
Axes of the slice: x: 4, y: 4, z: 32, core: 2. Of those that a mesh axis runs over, the one named last changes fastest.
Arguments:
- gradient: float32 [3, 16, 2048, 128], P(None, 'group', 'cuts'), may hold values from -6 to 6
- basis: bfloat16 [16, 2048, 128, 128], P('group', 'cuts'), may hold values from -0.5 to 0.5
- block_owner: int32 [16, 2048, 1], P('group', 'cuts'), may hold values from 0 to 63; in each aligned block of 32 rows (0 to 31, 32 to 63, ..., all dimensions but the last counted through in order) at most 2 rows name the same one
- block_local: int32 [16, 2048], P('group', 'cuts'), may hold values from 0 to 15
- valid_count: int32 [16, 2048], P('group', 'cuts'), may hold values from 32 to 128
- band_offsets: int32 [4], replicated, may hold values from -16 to 16
- band_weight: float32 [3, 4], replicated, may hold values from 0.02 to 0.12
- radial_weight: float32 [3], replicated, may hold values from 0.05 to 0.2
Outputs:
- smoothed_gradient: float32 [3, 16, 2048, 128], P(None, 'group', 'cuts')
The draws below stay inside these ranges and needn't reach their ends.
Inputs may be any that keep to these rules, and one draw needn't show every extreme that they name: `block_owner`: among the blocks of one device, at most 2 have the same owner, a bound that some of them reach.
All inputs are finite; a program needn't handle non-finite values.
Results may differ from the reference program's by a relative error of at most 0.0038.
Values may be sent and summed in bfloat16 or wider, within the bound.
No kernel may reach another device: no remote copies, remote signals or barrier semaphores. Data moves between devices by JAX's collectives and lax.ppermute only.
A program may use at most 32 MiB of HBM per device.

```python
import math
import jax
import jax.numpy as jnp
import numpy as np
from jax import lax

PARAMS = 3
PB = 128
K = 128
NB = 32
PD = 16
BANDS = 4
CAP = 2
ROWS = 16
BLOCKS = 2048
N_CUTS = 64


def touch_ends(drawn, rng, low, high):
    spot = [jax.random.randint(jax.random.fold_in(rng, axis), (), 0, length) for axis, length in enumerate(drawn.shape)]
    longest = drawn.shape.index(max(drawn.shape))
    next_to = spot[:longest] + [(spot[longest] + 1) % drawn.shape[longest]] + spot[longest + 1:]
    return drawn.at[tuple(spot)].set(low).at[tuple(next_to)].set(high)


def level_of(rng, shape, cuts, smallest, top_value):
    def one(dim, parts):
        heights = jax.random.uniform(jax.random.fold_in(jax.random.fold_in(rng, 6), dim), (parts,), jnp.float32, smallest / len(cuts), top_value / len(cuts))
        return jnp.repeat(jnp.exp(heights), shape[dim] // parts).reshape((-1,) + (1,) * (len(shape) - dim - 1))

    factor_of = one(*cuts[0])
    for cut in cuts[1:]:
        factor_of = factor_of * one(*cut)
    return factor_of


def deal_out(rng, own, number, rows, number_of, top, limit, skew):
    order = jax.random.permutation(rng, number_of)
    packed, common = shares(number_of, rows * top, limit, skew, True), shares(number_of, rows * top, limit, skew, False)
    places = jnp.arange(number_of)

    def named(tallies, turn):
        used = int((tallies > 0).sum())
        fixed = max(1, used // 4)
        moved = fixed + (places - fixed + turn * (used - fixed)) % max(1, number_of - fixed)
        return jnp.zeros((number_of,), jnp.int32).at[order[jnp.where(places < fixed, places, moved)]].set(jnp.asarray(tallies, jnp.int32))

    tallies = jnp.where(number % 4 == 0, named(packed, number // 4), named(common, number - number // 4 - 1))
    mixed = jax.random.permutation(jax.random.fold_in(own, 3), number_of)
    giver, taker = mixed[0:number_of // 2 * 2:2], mixed[1:number_of // 2 * 2:2]
    room = jnp.minimum(tallies[giver] - 1, limit - tallies[taker]) // 2
    room = jnp.where((giver == order[0]) | (taker == order[0]) | (tallies[taker] == 0), 0, jnp.maximum(room, 0))
    moved = jax.random.randint(jax.random.fold_in(own, 4), (number_of // 2,), 0, 1 << 20) % (room + 1)
    tallies = tallies.at[giver].add(-moved).at[taker].add(moved)
    members = jnp.searchsorted(jnp.cumsum(tallies), jnp.arange(rows * top), side="right").astype(jnp.int32)
    grid = members.reshape(top, rows).T
    grid = grid[jax.random.permutation(jax.random.fold_in(own, 1), rows)]
    turn = jax.random.randint(jax.random.fold_in(own, 2), (rows, 1), 0, top)
    return jnp.take_along_axis(grid, (jnp.arange(top)[None, :] + turn) % top, axis=1)


def shares(amount, total, limit, skew, full):
    weights = [(1 << 20) // math.isqrt(rank ** skew) + 1 for rank in range(1, amount + 1)]
    largest = limit if full else min(limit, max(-(-total // amount), total * weights[0] // sum(weights)))
    least = 1 if total - largest >= amount - 1 else 0
    counts, surplus = [largest] + [least] * (amount - 1), total - largest - least * (amount - 1)
    while surplus > 0:
        free = [i for i in range(1, amount) if counts[i] < largest] or [i for i in range(1, amount) if counts[i] < limit]
        mass, left = sum([weights[i] for i in free]), surplus
        for i in free:
            more = min(limit - counts[i], max(1, left * weights[i] // mass), surplus)
            counts[i] = counts[i] + more
            surplus = surplus - more
    return np.array(counts)


def bell_draw(own_key, dims, width, most, cuts=(), held_as=jnp.bfloat16):
    gain = level_of(own_key, dims, cuts, -0.22, 0.18) if cuts else 1.0
    array = jax.random.normal(own_key, dims, jnp.float32) * width * gain
    return jnp.minimum(jnp.maximum(array, -most), most).astype(held_as)


def setup_inputs(seed: int = 0) -> dict:
    seeds = jax.random.split(jax.random.key(seed), 9)
    gradient = bell_draw(seeds[0], (PARAMS, ROWS, BLOCKS, PB), 1.0, 6.0, ((1, 16), (2, 64)), jnp.float32)
    basis = bell_draw(seeds[1], (ROWS, BLOCKS, PB, K), K ** -0.5, 0.5, ((0, 16), (1, 64)))
    block_owner_keys = jax.random.split(jax.random.fold_in(seeds[2], 1), ROWS * BLOCKS // NB)
    block_owner_turns = jax.random.permutation(jax.random.fold_in(seeds[2], 3), ROWS * BLOCKS // NB)
    block_owner = jax.vmap(lambda own, number: deal_out(jax.random.fold_in(seeds[2], 2), own, number, NB, N_CUTS, 1, CAP, 2))(block_owner_keys, block_owner_turns).reshape((ROWS, BLOCKS, 1))
    block_local = touch_ends(jax.random.randint(seeds[3], (ROWS, BLOCKS), 0, PD), jax.random.fold_in(seeds[3], 1), 0, PD - 1).astype(jnp.int32)
    valid_count = touch_ends(jax.random.randint(seeds[4], (ROWS, BLOCKS), PB // 4, PB + 1), jax.random.fold_in(seeds[4], 1), PB // 4, PB).astype(jnp.int32)
    band_offsets = touch_ends(jax.random.randint(seeds[5], (BANDS,), 0 - PD, PD + 1), jax.random.fold_in(seeds[5], 1), 0 - PD, PD).astype(jnp.int32)
    band_weight = jnp.clip(jnp.exp(jax.random.uniform(seeds[6], (PARAMS, BANDS), jnp.float32, math.log(0.02), math.log(0.12))), 0.02, 0.12)
    radial_weight = jnp.clip(jnp.exp(jax.random.uniform(seeds[7], (PARAMS,), jnp.float32, math.log(0.05), math.log(0.2))), 0.05, 0.2)
    return {"gradient": gradient, "basis": basis, "block_owner": block_owner, "block_local": block_local, "valid_count": valid_count, "band_offsets": band_offsets, "band_weight": band_weight, "radial_weight": radial_weight}


def reference(gradient, basis, block_owner, block_local, valid_count, band_offsets, band_weight, radial_weight):
    patch_count = N_CUTS * PD
    points = jnp.arange(PB, dtype=jnp.int32)
    inside = points[None, None, :] < valid_count[:, :, None]
    masked_values = jnp.where(inside[None], gradient, 0.0).astype(jnp.bfloat16)
    patch_index = (block_owner[:, :, 0] * PD + block_local).astype(jnp.int32)
    columns = jnp.arange(patch_count, dtype=jnp.int32)

    def project(row_inputs):
        gradient_row, spline_basis_row, patch_row = row_inputs
        projected_gradient = jnp.einsum('xrg,rgv->rxv', gradient_row.astype(jnp.float32), spline_basis_row.astype(jnp.float32))
        onehot = (patch_row[:, None] == columns[None, :]).astype(jnp.float32)
        return jnp.einsum('bn,bpk->pnk', onehot, projected_gradient, precision=lax.Precision.HIGHEST)

    coefficients = lax.map(project, (jnp.transpose(masked_values, (1, 0, 2, 3)), basis, patch_index))
    lateral_sum = jnp.zeros_like(coefficients)
    for band_number_index in range(BANDS):
        shifted = jnp.roll(coefficients, -band_offsets[band_number_index], axis=2)
        lateral_sum = lateral_sum + band_weight[None, :, band_number_index, None, None] * (shifted - coefficients)
    zeros_row = jnp.zeros_like(coefficients[:1])
    outward = jnp.concatenate([coefficients[1:], zeros_row], axis=0)
    inward = jnp.concatenate([zeros_row, coefficients[:-1]], axis=0)
    radial_sum = radial_weight[None, :, None, None] * (outward + inward - 2.0 * coefficients)
    smooth = (coefficients + lateral_sum + radial_sum).astype(jnp.bfloat16)

    def expand(row_inputs):
        spline_basis_row, smooth_row, patch_row = row_inputs
        picked_rows = jnp.take(smooth_row, patch_row, axis=1)
        return jnp.einsum('jcm,ojm->ojc', spline_basis_row.astype(jnp.float32), picked_rows.astype(jnp.float32))

    broadcast_values = lax.map(expand, (basis, smooth, patch_index))
    broadcast_values = jnp.transpose(broadcast_values, (1, 0, 2, 3))
    return jnp.where(inside[None], broadcast_values, 0.0)
```

```python
import jax
import jax.numpy as jnp
from jax import lax
from jax.experimental import pallas as pl
from jax.experimental.pallas import tpu as pltpu
from jax.sharding import PartitionSpec as P

PD = 16
CORES = 2
ID_ROWS = 8


def column(row, count):
    lanes = row.shape[1]
    wide = jnp.broadcast_to(row, (count, lanes))
    at = lax.broadcasted_iota(jnp.int32, (count, lanes), 0) == lax.broadcasted_iota(
        jnp.int32, (count, lanes), 1
    )
    return jnp.sum(jnp.where(at, wide, 0), axis=1, keepdims=True)


def inside_mask(valid_ref, blocks, points):
    count = column(valid_ref[...], blocks)
    return lax.broadcasted_iota(jnp.int32, (blocks, points), 1) < count


def project_kernel(
    gradient_hbm, basis_hbm, patch_ref, valid_ref, payload_ref, gradient_ref, basis_ref, rows_ref, ids_ref, done
):
    copies = [
        pltpu.make_async_copy(gradient_hbm, gradient_ref, done.at[0]),
        pltpu.make_async_copy(basis_hbm, basis_ref, done.at[1]),
    ]
    for copy in copies:
        copy.start()
    params, _, blocks, points = gradient_ref.shape
    inside = inside_mask(valid_ref, blocks, points)
    ids_ref[...] = jnp.zeros_like(ids_ref)
    ids_ref[0:1, 0:blocks] = patch_ref[...] // PD
    ids_ref[1:2, 0:blocks] = patch_ref[...] % PD
    position = lax.axis_index("cuts")
    quarter = (position // (2 * CORES)) % 2 * CORES + position % CORES
    ids = pltpu.roll(ids_ref[...].astype(jnp.float32), quarter * blocks, 1)
    payload_ref[params * blocks :, :] = ids.astype(jnp.bfloat16)
    copies[0].wait()
    for p in range(params):
        rows_ref[p] = jnp.where(inside, gradient_ref[p, 0], 0.0)
    copies[1].wait()
    for b in range(blocks):
        masked = rows_ref[:, b, :].astype(jnp.bfloat16)
        rows_ref[:, b, :] = jnp.dot(masked, basis_ref[0, b], preferred_element_type=jnp.float32)
    for p in range(params):
        payload_ref[p * blocks : (p + 1) * blocks, :] = rows_ref[p].astype(jnp.bfloat16)


def patch_sums(wanted, all_ref, params, blocks):
    members, rows, width = all_ref.shape
    group = 128 // blocks
    tile = 2 * group
    total = jnp.zeros((wanted.shape[0], params * width), jnp.float32)
    for first in (0, rows // 2):
        marks = slice(first + params * blocks, first + rows // 2)
        for start in range(0, members, tile):
            ids = []
            for half in range(start, start + tile, group):
                ids.append(
                    sum(all_ref[m, marks, :].astype(jnp.float32) for m in range(half, half + group))
                )
            ids = jnp.concatenate(ids, axis=1)
            patch = (ids[0:1] * PD + ids[1:2]).astype(jnp.int32)
            hit = jnp.where(wanted == patch, 1.0, 0.0).astype(jnp.bfloat16)
            values = jnp.concatenate(
                [
                    jnp.concatenate(
                        [
                            all_ref[m, first + p * blocks : first + (p + 1) * blocks, :]
                            for m in range(start, start + tile)
                        ],
                        axis=0,
                    )
                    for p in range(params)
                ],
                axis=1,
            )
            total += jnp.dot(hit, values, preferred_element_type=jnp.float32)
    return total


def radial_kernel(up_ref, down_ref, all_ref, to_up_ref, to_down_ref):
    blocks = to_up_ref.shape[0]
    width = all_ref.shape[2]
    params = to_up_ref.shape[1] // width
    wanted = jnp.concatenate(
        [column(up_ref[...], blocks), column(down_ref[...], blocks)], axis=0
    )
    total = patch_sums(wanted, all_ref, params, blocks).astype(jnp.bfloat16)
    to_up_ref[...] = total[:blocks]
    to_down_ref[...] = total[blocks:]


def lateral_kernel(offsets_ref, band_ref, radial_ref, wants_ref, all_ref, out_ref):
    width = all_ref.shape[2]
    params, bands = band_ref.shape
    blocks = out_ref.shape[0] - 8
    patches = all_ref.shape[0] * 2 * PD
    mine = column(wants_ref[...], blocks)
    wanted = [mine]
    for j in range(bands):
        moved = mine + offsets_ref[j]
        moved = jnp.where(moved < 0, moved + patches, moved)
        wanted.append(jnp.where(moved >= patches, moved - patches, moved))
    total = patch_sums(jnp.concatenate(wanted, axis=0), all_ref, params, blocks)
    for p in range(params):
        part = total[:, p * width : (p + 1) * width]
        centre = part[:blocks]
        smooth = centre - (2.0 * radial_ref[p]) * centre
        for j in range(bands):
            shifted = part[(j + 1) * blocks : (j + 2) * blocks]
            smooth = smooth + band_ref[p, j] * (shifted - centre)
        out_ref[:blocks, p * width : (p + 1) * width] = smooth
        out_ref[blocks:, p * width : (p + 1) * width] = jnp.full((8, width), radial_ref[p], jnp.float32)


def expand_kernel(part_ref, up_ref, down_ref, basis_ref, valid_ref, out_ref, rows_ref):
    params, _, blocks, points = out_ref.shape
    width = basis_ref.shape[3]
    neighbours = up_ref[...].astype(jnp.float32) + down_ref[...].astype(jnp.float32)
    smooth = part_ref[:blocks] + part_ref[blocks : blocks + 1] * neighbours
    for p in range(params):
        rows_ref[p] = smooth[:, p * width : (p + 1) * width]
    for b in range(blocks):
        picked = rows_ref[:, b, :].astype(jnp.bfloat16)
        rows_ref[:, b, :] = lax.dot_general(
            picked, basis_ref[0, b], (((1,), (1,)), ((), ())), preferred_element_type=jnp.float32
        )
    inside = inside_mask(valid_ref, blocks, points)
    for p in range(params):
        out_ref[p, 0] = jnp.where(inside, rows_ref[p], 0.0)


VMEM = pl.BlockSpec(memory_space=pltpu.VMEM)
ANY = pl.BlockSpec(memory_space=pl.ANY)
SMEM = pl.BlockSpec(memory_space=pltpu.SMEM)


def call(kernel, ins, out_shape, flops, scratch=()):
    many = isinstance(out_shape, tuple)
    return pl.pallas_call(
        kernel,
        out_shape=out_shape,
        in_specs=list(ins),
        out_specs=(VMEM,) * len(out_shape) if many else VMEM,
        scratch_shapes=list(scratch),
        compiler_params=pltpu.CompilerParams(vmem_limit_bytes=24 * 2**20),
        cost_estimate=pl.CostEstimate(flops=flops, bytes_accessed=2**21, transcendentals=0),
    )


def body(
    gradient, basis, block_owner, block_local, valid_count, band_offsets, band_weight, radial_weight
):
    params, _, blocks, points = gradient.shape
    width = basis.shape[3]
    cuts, rows = lax.axis_size("cuts"), lax.axis_size("group")
    chips = cuts // CORES
    values = params * width
    wants = block_owner[:, :, 0] * PD + block_local
    higher = [(i, i + 1) for i in range(rows - 1)]
    lower = [(j, i) for i, j in higher]
    wants_of_lower = lax.ppermute(wants, "group", higher)
    wants_of_higher = lax.ppermute(wants, "group", lower)
    payload = call(
        project_kernel,
        [ANY] * 2 + [VMEM] * 2,
        jax.ShapeDtypeStruct((params * blocks + ID_ROWS, width), jnp.bfloat16),
        2 * blocks * params * points * width,
        [
            pltpu.VMEM(gradient.shape, gradient.dtype),
            pltpu.VMEM(basis.shape, basis.dtype),
            pltpu.VMEM((params, blocks, width), jnp.float32),
            pltpu.VMEM((ID_ROWS, 128), jnp.int32),
            pltpu.SemaphoreType.DMA((2,)),
        ],
    )(gradient, basis, wants, valid_count)
    partner = [(CORES * z + c, CORES * (z ^ 1) + c) for z in range(chips) for c in range(CORES)]
    pair = jnp.concatenate([payload, lax.ppermute(payload, "cuts", partner)])
    halves = [[CORES * z + c for z in range(h, chips, 2) for c in range(CORES)] for h in range(2)]
    everything = lax.all_gather(pair, "cuts", axis_index_groups=halves)
    piece = jax.ShapeDtypeStruct((blocks, values), jnp.bfloat16)
    to_higher, to_lower = call(
        radial_kernel, [VMEM] * 3, (piece, piece), 4 * blocks * blocks * cuts * values
    )(wants_of_higher, wants_of_lower, everything)
    from_lower = lax.ppermute(to_higher, "group", higher)
    from_higher = lax.ppermute(to_lower, "group", lower)
    part = call(
        lateral_kernel,
        [SMEM] * 3 + [VMEM] * 2,
        jax.ShapeDtypeStruct((blocks + 8, values), jnp.float32),
        10 * blocks * blocks * cuts * values,
    )(band_offsets, band_weight, radial_weight, wants, everything)
    return call(
        expand_kernel,
        [VMEM] * 5,
        jax.ShapeDtypeStruct((params, 1, blocks, points), jnp.float32),
        2 * blocks * params * points * width,
        [pltpu.VMEM((params, blocks, width), jnp.float32)],
    )(part, from_lower, from_higher, basis, valid_count)


def solution(mesh):
    return jax.shard_map(
        body,
        mesh=mesh,
        in_specs=(
            P(None, "group", "cuts", None),
            P("group", "cuts", None, None),
            P("group", "cuts", None),
            P("group", "cuts"),
            P("group", "cuts"),
            P(),
            P(),
            P(),
        ),
        out_specs=P(None, "group", "cuts", None),
        check_vma=False,
    )
```

```python
import jax
import jax.numpy as jnp
from jax import lax
from jax.experimental import pallas as pl
from jax.experimental.pallas import tpu as pltpu
from jax.sharding import PartitionSpec as P

PD = 16
CORES = 2
ID_ROWS = 8


def column(row, count):
    lanes = row.shape[1]
    wide = jnp.broadcast_to(row, (count, lanes))
    at = lax.broadcasted_iota(jnp.int32, (count, lanes), 0) == lax.broadcasted_iota(
        jnp.int32, (count, lanes), 1
    )
    return jnp.sum(jnp.where(at, wide, 0), axis=1, keepdims=True)


def inside_mask(valid_ref, blocks, points):
    count = column(valid_ref[...], blocks)
    return lax.broadcasted_iota(jnp.int32, (blocks, points), 1) < count


def project_kernel(
    gradient_hbm, basis_hbm, patch_ref, valid_ref, payload_ref, gradient_ref, basis_ref, rows_ref, ids_ref, done
):
    copies = [
        pltpu.make_async_copy(gradient_hbm, gradient_ref, done.at[0]),
        pltpu.make_async_copy(basis_hbm, basis_ref, done.at[1]),
    ]
    for copy in copies:
        copy.start()
    params, _, blocks, points = gradient_ref.shape
    inside = inside_mask(valid_ref, blocks, points)
    ids_ref[...] = jnp.zeros_like(ids_ref)
    ids_ref[0:1, 0:blocks] = patch_ref[...] // PD
    ids_ref[1:2, 0:blocks] = patch_ref[...] % PD
    position = lax.axis_index("cuts")
    quarter = (position // (2 * CORES)) % 2 * CORES + position % CORES
    ids = pltpu.roll(ids_ref[...].astype(jnp.float32), quarter * blocks, 1)
    payload_ref[params * blocks :, :] = ids.astype(jnp.bfloat16)
    copies[0].wait()
    for p in range(params):
        rows_ref[p] = jnp.where(inside, gradient_ref[p, 0], 0.0)
    copies[1].wait()
    for b in range(blocks):
        masked = rows_ref[:, b, :].astype(jnp.bfloat16)
        rows_ref[:, b, :] = jnp.dot(masked, basis_ref[0, b], preferred_element_type=jnp.float32)
    for p in range(params):
        payload_ref[p * blocks : (p + 1) * blocks, :] = rows_ref[p].astype(jnp.bfloat16)


def patch_sums(wanted, all_ref, params, blocks):
    members, _, width = all_ref.shape
    group = 128 // blocks
    tile = 2 * group
    total = jnp.zeros((wanted.shape[0], params * width), jnp.float32)
    for start in range(0, members, tile):
        ids = []
        for half in range(start, start + tile, group):
            ids.append(
                sum(all_ref[m, params * blocks :, :].astype(jnp.float32) for m in range(half, half + group))
            )
        ids = jnp.concatenate(ids, axis=1)
        patch = (ids[0:1] * PD + ids[1:2]).astype(jnp.int32)
        hit = jnp.where(wanted == patch, 1.0, 0.0).astype(jnp.bfloat16)
        values = jnp.concatenate(
            [
                jnp.concatenate(
                    [all_ref[m, p * blocks : (p + 1) * blocks, :] for m in range(start, start + tile)],
                    axis=0,
                )
                for p in range(params)
            ],
            axis=1,
        )
        total += jnp.dot(hit, values, preferred_element_type=jnp.float32)
    return total


def columns(ref, blocks):
    return [column(ref[i : i + 1, :], blocks) for i in range(ref.shape[0])]


def radial_kernel(up_ref, down_ref, all_ref, to_up_ref, to_down_ref):
    count = to_up_ref.shape[0]
    blocks = count // up_ref.shape[0]
    params = to_up_ref.shape[1] // all_ref.shape[2]
    wanted = jnp.concatenate(columns(up_ref, blocks) + columns(down_ref, blocks), axis=0)
    total = patch_sums(wanted, all_ref, params, blocks).astype(jnp.bfloat16)
    to_up_ref[...] = total[:count]
    to_down_ref[...] = total[count:]


def lateral_kernel(offsets_ref, band_ref, radial_ref, wants_ref, all_ref, out_ref):
    width = all_ref.shape[2]
    params, bands = band_ref.shape
    count = out_ref.shape[0] - 8
    blocks = count // wants_ref.shape[0]
    patches = all_ref.shape[0] * 2 * PD
    mine = jnp.concatenate(columns(wants_ref, blocks), axis=0)
    wanted = [mine]
    for j in range(bands):
        moved = mine + offsets_ref[j]
        moved = jnp.where(moved < 0, moved + patches, moved)
        wanted.append(jnp.where(moved >= patches, moved - patches, moved))
    total = patch_sums(jnp.concatenate(wanted, axis=0), all_ref, params, blocks)
    for p in range(params):
        part = total[:, p * width : (p + 1) * width]
        centre = part[:count]
        smooth = centre - (2.0 * radial_ref[p]) * centre
        for j in range(bands):
            shifted = part[(j + 1) * count : (j + 2) * count]
            smooth = smooth + band_ref[p, j] * (shifted - centre)
        out_ref[:count, p * width : (p + 1) * width] = smooth
        out_ref[count:, p * width : (p + 1) * width] = jnp.full((8, width), radial_ref[p], jnp.float32)


def radial_added(part_ref, up_ref, down_ref, first, blocks):
    count = up_ref.shape[0]
    rows = slice(first, first + blocks)
    neighbours = up_ref[rows, :].astype(jnp.float32) + down_ref[rows, :].astype(jnp.float32)
    return part_ref[rows, :] + part_ref[count : count + 1, :] * neighbours


def partner_kernel(part_ref, up_ref, down_ref, out_ref):
    blocks = out_ref.shape[0]
    out_ref[...] = radial_added(part_ref, up_ref, down_ref, blocks, blocks).astype(out_ref.dtype)


def expand_kernel(part_ref, up_ref, down_ref, other_ref, basis_ref, valid_ref, out_ref, rows_ref):
    params, _, blocks, points = out_ref.shape
    width = basis_ref.shape[3]
    smooth = radial_added(part_ref, up_ref, down_ref, 0, blocks) + other_ref[...].astype(jnp.float32)
    for p in range(params):
        rows_ref[p] = smooth[:, p * width : (p + 1) * width]
    for b in range(blocks):
        picked = rows_ref[:, b, :].astype(jnp.bfloat16)
        rows_ref[:, b, :] = lax.dot_general(
            picked, basis_ref[0, b], (((1,), (1,)), ((), ())), preferred_element_type=jnp.float32
        )
    inside = inside_mask(valid_ref, blocks, points)
    for p in range(params):
        out_ref[p, 0] = jnp.where(inside, rows_ref[p], 0.0)


VMEM = pl.BlockSpec(memory_space=pltpu.VMEM)
HBM = pl.BlockSpec(memory_space=pltpu.HBM)
SMEM = pl.BlockSpec(memory_space=pltpu.SMEM)


def call(kernel, ins, out_shape, flops, scratch=()):
    many = isinstance(out_shape, tuple)
    return pl.pallas_call(
        kernel,
        out_shape=out_shape,
        in_specs=list(ins),
        out_specs=(VMEM,) * len(out_shape) if many else VMEM,
        scratch_shapes=list(scratch),
        compiler_params=pltpu.CompilerParams(vmem_limit_bytes=24 * 2**20),
        cost_estimate=pl.CostEstimate(flops=flops, bytes_accessed=2**21, transcendentals=0),
    )


def body(
    gradient, basis, block_owner, block_local, valid_count, band_offsets, band_weight, radial_weight
):
    params, _, blocks, points = gradient.shape
    width = basis.shape[3]
    cuts, rows = lax.axis_size("cuts"), lax.axis_size("group")
    chips = cuts // CORES
    values = params * width
    partner = [(CORES * z + c, CORES * (z ^ 1) + c) for z in range(chips) for c in range(CORES)]
    higher = [(i, i + 1) for i in range(rows - 1)]
    lower = [(j, i) for i, j in higher]
    own = block_owner[:, :, 0] * PD + block_local
    wants = jnp.concatenate([own, lax.ppermute(own, "cuts", partner)])
    wants_of_lower = lax.ppermute(wants, "group", higher)
    wants_of_higher = lax.ppermute(wants, "group", lower)
    payload = call(
        project_kernel,
        [HBM] * 2 + [VMEM] * 2,
        jax.ShapeDtypeStruct((params * blocks + ID_ROWS, width), jnp.bfloat16),
        2 * blocks * params * points * width,
        [
            pltpu.VMEM(gradient.shape, gradient.dtype),
            pltpu.VMEM(basis.shape, basis.dtype),
            pltpu.VMEM((params, blocks, width), jnp.float32),
            pltpu.VMEM((ID_ROWS, 128), jnp.int32),
            pltpu.SemaphoreType.DMA((2,)),
        ],
    )(gradient, basis, own, valid_count)
    halves = [[CORES * z + c for z in range(h, chips, 2) for c in range(CORES)] for h in range(2)]
    gathered = lax.all_gather(payload, "cuts", axis_index_groups=halves)
    piece = jax.ShapeDtypeStruct((2 * blocks, values), jnp.bfloat16)
    one_hot = blocks * blocks * cuts * values
    to_higher, to_lower = call(radial_kernel, [VMEM] * 3, (piece, piece), 4 * one_hot)(
        wants_of_higher, wants_of_lower, gathered
    )
    from_lower = lax.ppermute(to_higher, "group", higher)
    from_higher = lax.ppermute(to_lower, "group", lower)
    part = call(
        lateral_kernel,
        [SMEM] * 3 + [VMEM] * 2,
        jax.ShapeDtypeStruct((2 * blocks + 8, values), jnp.float32),
        10 * one_hot,
    )(band_offsets, band_weight, radial_weight, wants, gathered)
    for_partner = call(
        partner_kernel, [VMEM] * 3, jax.ShapeDtypeStruct((blocks, values), jnp.bfloat16), blocks * values
    )(part, from_lower, from_higher)
    from_partner = lax.ppermute(for_partner, "cuts", partner)
    return call(
        expand_kernel,
        [VMEM] * 6,
        jax.ShapeDtypeStruct((params, 1, blocks, points), jnp.float32),
        2 * blocks * params * points * width,
        [pltpu.VMEM((params, blocks, width), jnp.float32)],
    )(part, from_lower, from_higher, from_partner, basis, valid_count)


def solution(mesh):
    return jax.shard_map(
        body,
        mesh=mesh,
        in_specs=(
            P(None, "group", "cuts", None),
            P("group", "cuts", None, None),
            P("group", "cuts", None),
            P("group", "cuts"),
            P("group", "cuts"),
            P(),
            P(),
            P(),
        ),
        out_specs=P(None, "group", "cuts", None),
        check_vma=False,
    )
```

```python
import jax
import jax.numpy as jnp
from jax import lax
from jax.experimental import pallas as pl
from jax.experimental.pallas import tpu as pltpu
from jax.sharding import PartitionSpec as P

PD = 16
CORES = 2
ID_ROWS = 8


def column(row, count):
    lanes = row.shape[1]
    wide = jnp.broadcast_to(row, (count, lanes))
    at = lax.broadcasted_iota(jnp.int32, (count, lanes), 0) == lax.broadcasted_iota(
        jnp.int32, (count, lanes), 1
    )
    return jnp.sum(jnp.where(at, wide, 0), axis=1, keepdims=True)


def inside_mask(valid_ref, blocks, points):
    count = column(valid_ref[...], blocks)
    return lax.broadcasted_iota(jnp.int32, (blocks, points), 1) < count


def quarter(position):
    return (position // (2 * CORES)) % 2 * CORES + position % CORES


def project_kernel(
    gradient_hbm, basis_hbm, patch_ref, valid_ref, other_ref, up_ref, down_ref, payload_ref, known_ref, gradient_ref, basis_ref, rows_ref, ids_ref, done
):
    copies = [
        pltpu.make_async_copy(gradient_hbm, gradient_ref, done.at[0]),
        pltpu.make_async_copy(basis_hbm, basis_ref, done.at[1]),
    ]
    for copy in copies:
        copy.start()
    params, _, blocks, points = gradient_ref.shape
    inside = inside_mask(valid_ref, blocks, points)
    ids_ref[...] = jnp.zeros_like(ids_ref)
    ids_ref[0:1, 0:blocks] = patch_ref[...] // PD
    ids_ref[1:2, 0:blocks] = patch_ref[...] % PD
    known_ref[0:1, :] = patch_ref[...]
    known_ref[1:2, :] = other_ref[...]
    known_ref[2:4, :] = up_ref[...]
    known_ref[4:6, :] = down_ref[...]
    known_ref[6:8, :] = jnp.zeros_like(down_ref)
    ids = pltpu.roll(ids_ref[...].astype(jnp.float32), quarter(lax.axis_index("cuts")) * blocks, 1)
    payload_ref[params * blocks :, :] = ids.astype(jnp.bfloat16)
    copies[0].wait()
    for p in range(params):
        rows_ref[p] = jnp.where(inside, gradient_ref[p, 0], 0.0)
    copies[1].wait()
    for b in range(blocks):
        masked = rows_ref[:, b, :].astype(jnp.bfloat16)
        rows_ref[:, b, :] = jnp.dot(masked, basis_ref[0, b], preferred_element_type=jnp.float32)
    for p in range(params):
        payload_ref[p * blocks : (p + 1) * blocks, :] = rows_ref[p].astype(jnp.bfloat16)


def patch_sums(wanted, all_ref, params, blocks):
    members, _, width = all_ref.shape
    group = 128 // blocks
    tile = 2 * group
    total = jnp.zeros((wanted.shape[0], params * width), jnp.float32)
    for start in range(0, members, tile):
        ids = []
        for half in range(start, start + tile, group):
            ids.append(
                sum(all_ref[m, params * blocks :, :].astype(jnp.float32) for m in range(half, half + group))
            )
        ids = jnp.concatenate(ids, axis=1)
        patch = (ids[0:1] * PD + ids[1:2]).astype(jnp.int32)
        hit = jnp.where(wanted == patch, 1.0, 0.0).astype(jnp.bfloat16)
        values = jnp.concatenate(
            [
                jnp.concatenate(
                    [all_ref[m, p * blocks : (p + 1) * blocks, :] for m in range(start, start + tile)],
                    axis=0,
                )
                for p in range(params)
            ],
            axis=1,
        )
        total += jnp.dot(hit, values, preferred_element_type=jnp.float32)
    return total


def columns(known_ref, late_ref, first, count, blocks):
    ids = known_ref[first : first + count, :] + late_ref[...]
    return jnp.concatenate([column(ids[i : i + 1], blocks) for i in range(count)], axis=0)


def radial_kernel(known_ref, late_up_ref, late_down_ref, all_ref, to_up_ref, to_down_ref):
    count = to_up_ref.shape[0]
    blocks = count // 2
    params = to_up_ref.shape[1] // all_ref.shape[2]
    wanted = jnp.concatenate(
        [columns(known_ref, late_up_ref, 2, 2, blocks), columns(known_ref, late_down_ref, 4, 2, blocks)],
        axis=0,
    )
    total = patch_sums(wanted, all_ref, params, blocks).astype(jnp.bfloat16)
    to_up_ref[...] = total[:count]
    to_down_ref[...] = total[count:]


def lateral_kernel(offsets_ref, band_ref, radial_ref, known_ref, late_other_ref, all_ref, out_ref):
    width = all_ref.shape[2]
    params, bands = band_ref.shape
    count = out_ref.shape[0] - 8
    blocks = count // 2
    patches = all_ref.shape[0] * 2 * PD
    mine = jnp.concatenate(
        [column(known_ref[0:1, :], blocks), columns(known_ref, late_other_ref, 1, 1, blocks)], axis=0
    )
    wanted = [mine]
    for j in range(bands):
        moved = mine + offsets_ref[j]
        moved = jnp.where(moved < 0, moved + patches, moved)
        wanted.append(jnp.where(moved >= patches, moved - patches, moved))
    total = patch_sums(jnp.concatenate(wanted, axis=0), all_ref, params, blocks)
    for p in range(params):
        part = total[:, p * width : (p + 1) * width]
        centre = part[:count]
        smooth = centre - (2.0 * radial_ref[p]) * centre
        for j in range(bands):
            shifted = part[(j + 1) * count : (j + 2) * count]
            smooth = smooth + band_ref[p, j] * (shifted - centre)
        out_ref[:count, p * width : (p + 1) * width] = smooth
        out_ref[count:, p * width : (p + 1) * width] = jnp.full((8, width), radial_ref[p], jnp.float32)


def radial_added(part_ref, up_ref, down_ref, first, blocks):
    count = up_ref.shape[0]
    rows = slice(first, first + blocks)
    neighbours = up_ref[rows, :].astype(jnp.float32) + down_ref[rows, :].astype(jnp.float32)
    return part_ref[rows, :] + part_ref[count : count + 1, :] * neighbours


def partner_kernel(part_ref, up_ref, down_ref, out_ref):
    blocks = out_ref.shape[0]
    out_ref[...] = radial_added(part_ref, up_ref, down_ref, blocks, blocks).astype(out_ref.dtype)


def expand_kernel(part_ref, up_ref, down_ref, other_ref, basis_ref, valid_ref, out_ref, rows_ref):
    params, _, blocks, points = out_ref.shape
    width = basis_ref.shape[3]
    smooth = radial_added(part_ref, up_ref, down_ref, 0, blocks) + other_ref[...].astype(jnp.float32)
    for p in range(params):
        rows_ref[p] = smooth[:, p * width : (p + 1) * width]
    for b in range(blocks):
        picked = rows_ref[:, b, :].astype(jnp.bfloat16)
        rows_ref[:, b, :] = lax.dot_general(
            picked, basis_ref[0, b], (((1,), (1,)), ((), ())), preferred_element_type=jnp.float32
        )
    inside = inside_mask(valid_ref, blocks, points)
    for p in range(params):
        out_ref[p, 0] = jnp.where(inside, rows_ref[p], 0.0)


VMEM = pl.BlockSpec(memory_space=pltpu.VMEM)
HBM = pl.BlockSpec(memory_space=pltpu.HBM)
SMEM = pl.BlockSpec(memory_space=pltpu.SMEM)


def call(kernel, ins, out_shape, flops, scratch=()):
    many = isinstance(out_shape, tuple)
    return pl.pallas_call(
        kernel,
        out_shape=out_shape,
        in_specs=list(ins),
        out_specs=(VMEM,) * len(out_shape) if many else VMEM,
        scratch_shapes=list(scratch),
        compiler_params=pltpu.CompilerParams(vmem_limit_bytes=24 * 2**20),
        cost_estimate=pl.CostEstimate(flops=flops, bytes_accessed=2**21, transcendentals=0),
    )


def body(
    gradient, basis, block_owner, block_local, valid_count, band_offsets, band_weight, radial_weight
):
    params, _, blocks, points = gradient.shape
    width = basis.shape[3]
    cuts, rows = lax.axis_size("cuts"), lax.axis_size("group")
    chips = cuts // CORES
    values = params * width
    axes = ("group", "cuts")

    def permute(value, chosen, rise, flip):
        pairs = [
            (r * cuts + CORES * z + c, (r + rise) * cuts + CORES * (z ^ flip) + c)
            for r in range(max(0, -rise), min(rows, rows - rise))
            for z in chosen
            for c in range(CORES)
        ]
        return lax.ppermute(value, axes, pairs)

    def wanted_near(own, chosen):
        other = permute(own, chosen, 0, 1)
        both = jnp.concatenate([own, other])
        return other, permute(both, chosen, -1, 0), permute(both, chosen, 1, 0)

    first, last = range(chips // 4), range(chips // 4, chips)
    own = block_owner[:, :, 0] * PD + block_local
    payload, known = call(
        project_kernel,
        [HBM] * 2 + [VMEM] * 5,
        (
            jax.ShapeDtypeStruct((params * blocks + ID_ROWS, width), jnp.bfloat16),
            jax.ShapeDtypeStruct((8, blocks), jnp.int32),
        ),
        2 * blocks * params * points * width,
        [
            pltpu.VMEM(gradient.shape, gradient.dtype),
            pltpu.VMEM(basis.shape, basis.dtype),
            pltpu.VMEM((params, blocks, width), jnp.float32),
            pltpu.VMEM((ID_ROWS, 128), jnp.int32),
            pltpu.SemaphoreType.DMA((2,)),
        ],
    )(gradient, basis, own, valid_count, *wanted_near(own, first))
    halves = [[CORES * z + c for z in range(h, chips, 2) for c in range(CORES)] for h in range(2)]
    gathered = lax.all_gather(payload, "cuts", axis_index_groups=halves)
    position = lax.axis_index("cuts")
    mine = lax.dynamic_slice(
        gathered,
        (position // (2 * CORES) * CORES + position % CORES, params * blocks, quarter(position) * blocks),
        (1, 2, blocks),
    )[0].astype(jnp.int32)
    late_other, late_higher, late_lower = wanted_near(mine[0:1] * PD + mine[1:2], last)
    piece = jax.ShapeDtypeStruct((2 * blocks, values), jnp.bfloat16)
    one_hot = blocks * blocks * cuts * values
    to_higher, to_lower = call(radial_kernel, [VMEM] * 4, (piece, piece), 4 * one_hot)(
        known, late_higher, late_lower, gathered
    )
    from_lower = permute(to_higher, range(chips), 1, 0)
    from_higher = permute(to_lower, range(chips), -1, 0)
    part = call(
        lateral_kernel,
        [SMEM] * 3 + [VMEM] * 3,
        jax.ShapeDtypeStruct((2 * blocks + 8, values), jnp.float32),
        10 * one_hot,
    )(band_offsets, band_weight, radial_weight, known, late_other, gathered)
    for_partner = call(
        partner_kernel, [VMEM] * 3, jax.ShapeDtypeStruct((blocks, values), jnp.bfloat16), blocks * values
    )(part, from_lower, from_higher)
    from_partner = permute(for_partner, range(chips), 0, 1)
    return call(
        expand_kernel,
        [VMEM] * 6,
        jax.ShapeDtypeStruct((params, 1, blocks, points), jnp.float32),
        2 * blocks * params * points * width,
        [pltpu.VMEM((params, blocks, width), jnp.float32)],
    )(part, from_lower, from_higher, from_partner, basis, valid_count)


def solution(mesh):
    return jax.shard_map(
        body,
        mesh=mesh,
        in_specs=(
            P(None, "group", "cuts", None),
            P("group", "cuts", None, None),
            P("group", "cuts", None),
            P("group", "cuts"),
            P("group", "cuts"),
            P(),
            P(),
            P(),
        ),
        out_specs=P(None, "group", "cuts", None),
        check_vma=False,
    )
```

```python
import jax
import jax.numpy as jnp
from jax import lax
from jax.experimental import pallas as pl
from jax.experimental.pallas import tpu as pltpu
from jax.sharding import PartitionSpec as P

PD = 16
CORES = 2
NEAR = 4
ID_ROWS = 8


def column(row, count):
    lanes = row.shape[1]
    wide = jnp.broadcast_to(row, (count, lanes))
    at = lax.broadcasted_iota(jnp.int32, (count, lanes), 0) == lax.broadcasted_iota(
        jnp.int32, (count, lanes), 1
    )
    return jnp.sum(jnp.where(at, wide, 0), axis=1, keepdims=True)


def inside_mask(valid_ref, blocks, points):
    count = column(valid_ref[...], blocks)
    return lax.broadcasted_iota(jnp.int32, (blocks, points), 1) < count


def project_kernel(
    gradient_hbm, basis_hbm, patch_ref, valid_ref, payload_ref, gradient_ref, basis_ref, rows_ref, ids_ref, done
):
    copies = [
        pltpu.make_async_copy(gradient_hbm, gradient_ref, done.at[0]),
        pltpu.make_async_copy(basis_hbm, basis_ref, done.at[1]),
    ]
    for copy in copies:
        copy.start()
    params, _, blocks, points = gradient_ref.shape
    inside = inside_mask(valid_ref, blocks, points)
    ids_ref[...] = jnp.zeros_like(ids_ref)
    ids_ref[0:1, 0:blocks] = patch_ref[0:1, :] // PD
    ids_ref[1:2, 0:blocks] = patch_ref[0:1, :] % PD
    position = lax.axis_index("cuts")
    quarter = (position // (NEAR * CORES)) % 2 * CORES + position % CORES
    ids = pltpu.roll(ids_ref[...].astype(jnp.float32), quarter * blocks, 1)
    payload_ref[params * blocks :, :] = ids.astype(jnp.bfloat16)
    copies[0].wait()
    for p in range(params):
        rows_ref[p] = jnp.where(inside, gradient_ref[p, 0], 0.0)
    copies[1].wait()
    for b in range(blocks):
        masked = rows_ref[:, b, :].astype(jnp.bfloat16)
        rows_ref[:, b, :] = jnp.dot(masked, basis_ref[0, b], preferred_element_type=jnp.float32)
    for p in range(params):
        payload_ref[p * blocks : (p + 1) * blocks, :] = rows_ref[p].astype(jnp.bfloat16)


def patch_sums(wanted, all_ref, params, blocks):
    members, _, width = all_ref.shape
    group = 128 // blocks
    tile = 2 * group
    total = jnp.zeros((wanted.shape[0], params * width), jnp.float32)
    for start in range(0, members, tile):
        ids = []
        for half in range(start, start + tile, group):
            ids.append(
                sum(all_ref[m, params * blocks :, :].astype(jnp.float32) for m in range(half, half + group))
            )
        ids = jnp.concatenate(ids, axis=1)
        patch = (ids[0:1] * PD + ids[1:2]).astype(jnp.int32)
        hit = jnp.where(wanted == patch, 1.0, 0.0).astype(jnp.bfloat16)
        values = jnp.concatenate(
            [
                jnp.concatenate(
                    [all_ref[m, p * blocks : (p + 1) * blocks, :] for m in range(start, start + tile)],
                    axis=0,
                )
                for p in range(params)
            ],
            axis=1,
        )
        total += jnp.dot(hit, values, preferred_element_type=jnp.float32)
    return total


def columns(ref, blocks):
    return [column(ref[i : i + 1, :], blocks) for i in range(ref.shape[0])]


def radial_kernel(up_ref, down_ref, all_ref, to_up_ref, to_down_ref):
    count = to_up_ref.shape[0]
    blocks = count // up_ref.shape[0]
    params = to_up_ref.shape[1] // all_ref.shape[2]
    wanted = jnp.concatenate(columns(up_ref, blocks) + columns(down_ref, blocks), axis=0)
    total = patch_sums(wanted, all_ref, params, blocks).astype(jnp.bfloat16)
    to_up_ref[...] = total[:count]
    to_down_ref[...] = total[count:]


def lateral_kernel(offsets_ref, band_ref, radial_ref, wants_ref, all_ref, basis_ref, out_ref, turned_ref):
    for b in range(turned_ref.shape[0]):
        turned_ref[b] = basis_ref[0, b].T
    width = all_ref.shape[2]
    params, bands = band_ref.shape
    count = out_ref.shape[0] - 8
    blocks = count // NEAR
    patches = all_ref.shape[0] * NEAR * PD
    mine = jnp.concatenate(columns(wants_ref, blocks), axis=0)
    wanted = [mine]
    for j in range(bands):
        moved = mine + offsets_ref[j]
        moved = jnp.where(moved < 0, moved + patches, moved)
        wanted.append(jnp.where(moved >= patches, moved - patches, moved))
    total = patch_sums(jnp.concatenate(wanted, axis=0), all_ref, params, blocks)
    for p in range(params):
        part = total[:, p * width : (p + 1) * width]
        centre = part[:count]
        smooth = centre - (2.0 * radial_ref[p]) * centre
        for j in range(bands):
            shifted = part[(j + 1) * count : (j + 2) * count]
            smooth = smooth + band_ref[p, j] * (shifted - centre)
        out_ref[:count, p * width : (p + 1) * width] = smooth
        out_ref[count:, p * width : (p + 1) * width] = jnp.full((8, width), radial_ref[p], jnp.float32)


def near_kernel(part_ref, up_ref, down_ref, out_ref):
    _, blocks, _ = out_ref.shape
    count = up_ref.shape[0]
    for i in range(NEAR):
        rows = slice(i * blocks, (i + 1) * blocks)
        neighbours = up_ref[rows, :].astype(jnp.float32) + down_ref[rows, :].astype(jnp.float32)
        out_ref[i] = (part_ref[rows, :] + part_ref[count : count + 1, :] * neighbours).astype(out_ref.dtype)


def expand_kernel(parts_ref, turned_ref, valid_ref, out_ref, rows_ref):
    params, _, blocks, points = out_ref.shape
    width = turned_ref.shape[1]
    smooth = sum(parts_ref[i].astype(jnp.float32) for i in range(NEAR))
    for p in range(params):
        rows_ref[p] = smooth[:, p * width : (p + 1) * width]
    for b in range(blocks):
        picked = rows_ref[:, b, :].astype(jnp.bfloat16)
        rows_ref[:, b, :] = jnp.dot(picked, turned_ref[b], preferred_element_type=jnp.float32)
    inside = inside_mask(valid_ref, blocks, points)
    for p in range(params):
        out_ref[p, 0] = jnp.where(inside, rows_ref[p], 0.0)


VMEM = pl.BlockSpec(memory_space=pltpu.VMEM)
HBM = pl.BlockSpec(memory_space=pltpu.HBM)
SMEM = pl.BlockSpec(memory_space=pltpu.SMEM)


def call(kernel, ins, out_shape, flops, scratch=()):
    many = isinstance(out_shape, tuple)
    return pl.pallas_call(
        kernel,
        out_shape=out_shape,
        in_specs=list(ins),
        out_specs=(VMEM,) * len(out_shape) if many else VMEM,
        scratch_shapes=list(scratch),
        compiler_params=pltpu.CompilerParams(vmem_limit_bytes=24 * 2**20),
        cost_estimate=pl.CostEstimate(flops=flops, bytes_accessed=2**21, transcendentals=0),
    )


def body(
    gradient, basis, block_owner, block_local, valid_count, band_offsets, band_weight, radial_weight
):
    params, _, blocks, points = gradient.shape
    width = basis.shape[3]
    cuts, rows = lax.axis_size("cuts"), lax.axis_size("group")
    chips = cuts // CORES
    values = params * width
    sets = [
        [CORES * (first + i) + c for i in range(NEAR)]
        for first in range(0, chips, NEAR)
        for c in range(CORES)
    ]
    higher = [(i, i + 1) for i in range(rows - 1)]
    lower = [(j, i) for i, j in higher]
    copies = (NEAR, blocks)
    own = jnp.broadcast_to(block_owner[:, :, 0], copies) * PD + jnp.broadcast_to(block_local, copies)
    wants = lax.all_to_all(own, "cuts", 0, 0, axis_index_groups=sets, tiled=True)
    wants_of_lower = lax.ppermute(wants, "group", higher)
    wants_of_higher = lax.ppermute(wants, "group", lower)
    payload = call(
        project_kernel,
        [HBM] * 2 + [VMEM] * 2,
        jax.ShapeDtypeStruct((params * blocks + ID_ROWS, width), jnp.bfloat16),
        2 * blocks * params * points * width,
        [
            pltpu.VMEM(gradient.shape, gradient.dtype),
            pltpu.VMEM(basis.shape, basis.dtype),
            pltpu.VMEM((params, blocks, width), jnp.float32),
            pltpu.VMEM((ID_ROWS, 128), jnp.int32),
            pltpu.SemaphoreType.DMA((2,)),
        ],
    )(gradient, basis, own, valid_count)
    shares = [
        [CORES * z + c for z in range(first, chips, NEAR) for c in range(CORES)] for first in range(NEAR)
    ]
    gathered = lax.all_gather(payload, "cuts", axis_index_groups=shares)
    piece = jax.ShapeDtypeStruct((NEAR * blocks, values), jnp.bfloat16)
    one_hot = blocks * blocks * cuts * values
    to_higher, to_lower = call(radial_kernel, [VMEM] * 3, (piece, piece), 4 * one_hot)(
        wants_of_higher, wants_of_lower, gathered
    )
    from_lower = lax.ppermute(to_higher, "group", higher)
    from_higher = lax.ppermute(to_lower, "group", lower)
    part, turned = call(
        lateral_kernel,
        [SMEM] * 3 + [VMEM] * 3,
        (
            jax.ShapeDtypeStruct((NEAR * blocks + 8, values), jnp.float32),
            jax.ShapeDtypeStruct((blocks, width, points), basis.dtype),
        ),
        10 * one_hot,
    )(band_offsets, band_weight, radial_weight, wants, gathered, basis)
    for_near = call(
        near_kernel,
        [VMEM] * 3,
        jax.ShapeDtypeStruct((NEAR, blocks, values), jnp.bfloat16),
        NEAR * blocks * values,
    )(part, from_lower, from_higher)
    parts = lax.all_to_all(for_near, "cuts", 0, 0, axis_index_groups=sets, tiled=True)
    return call(
        expand_kernel,
        [VMEM] * 3,
        jax.ShapeDtypeStruct((params, 1, blocks, points), jnp.float32),
        2 * blocks * params * points * width,
        [pltpu.VMEM((params, blocks, width), jnp.float32)],
    )(parts, turned, valid_count)


def solution(mesh):
    return jax.shard_map(
        body,
        mesh=mesh,
        in_specs=(
            P(None, "group", "cuts", None),
            P("group", "cuts", None, None),
            P("group", "cuts", None),
            P("group", "cuts"),
            P("group", "cuts"),
            P(),
            P(),
            P(),
        ),
        out_specs=P(None, "group", "cuts", None),
        check_vma=False,
    )
```

```python
import jax
import jax.numpy as jnp
from jax import lax
from jax.experimental import pallas as pl
from jax.experimental.pallas import tpu as pltpu
from jax.sharding import PartitionSpec as P

PD = 16
CORES = 2
NEAR = 4
ID_ROWS = 8


def column(row, count):
    lanes = row.shape[1]
    wide = jnp.broadcast_to(row, (count, lanes))
    at = lax.broadcasted_iota(jnp.int32, (count, lanes), 0) == lax.broadcasted_iota(
        jnp.int32, (count, lanes), 1
    )
    return jnp.sum(jnp.where(at, wide, 0), axis=1, keepdims=True)


def inside_mask(valid_ref, blocks, points):
    count = column(valid_ref[...], blocks)
    return lax.broadcasted_iota(jnp.int32, (blocks, points), 1) < count


def project_kernel(
    gradient_hbm, basis_hbm, patch_ref, valid_ref, payload_ref, gradient_ref, basis_ref, rows_ref, ids_ref, done
):
    copies = [
        pltpu.make_async_copy(gradient_hbm, gradient_ref, done.at[0]),
        pltpu.make_async_copy(basis_hbm, basis_ref, done.at[1]),
    ]
    for copy in copies:
        copy.start()
    params, _, blocks, points = gradient_ref.shape
    inside = inside_mask(valid_ref, blocks, points)
    ids_ref[...] = jnp.zeros_like(ids_ref)
    ids_ref[0:1, 0:blocks] = patch_ref[0:1, :] // PD
    ids_ref[1:2, 0:blocks] = patch_ref[0:1, :] % PD
    position = lax.axis_index("cuts")
    quarter = (position // (NEAR * CORES)) % 2 * CORES + position % CORES
    ids = pltpu.roll(ids_ref[...].astype(jnp.float32), quarter * blocks, 1)
    payload_ref[params * blocks :, :] = ids.astype(jnp.bfloat16)
    copies[0].wait()
    for p in range(params):
        rows_ref[p] = jnp.where(inside, gradient_ref[p, 0], 0.0)
    copies[1].wait()
    for b in range(blocks):
        masked = rows_ref[:, b, :].astype(jnp.bfloat16)
        rows_ref[:, b, :] = jnp.dot(masked, basis_ref[0, b], preferred_element_type=jnp.float32)
    for p in range(params):
        payload_ref[p * blocks : (p + 1) * blocks, :] = rows_ref[p].astype(jnp.bfloat16)


def patch_sums(wanted, all_ref, params, blocks):
    members, _, width = all_ref.shape
    group = 128 // blocks
    tile = 2 * group
    total = jnp.zeros((wanted.shape[0], params * width), jnp.float32)
    for start in range(0, members, tile):
        ids = []
        for half in range(start, start + tile, group):
            ids.append(
                sum(all_ref[m, params * blocks :, :].astype(jnp.float32) for m in range(half, half + group))
            )
        ids = jnp.concatenate(ids, axis=1)
        patch = (ids[0:1] * PD + ids[1:2]).astype(jnp.int32)
        hit = jnp.where(wanted == patch, 1.0, 0.0).astype(jnp.bfloat16)
        values = jnp.concatenate(
            [
                jnp.concatenate(
                    [all_ref[m, p * blocks : (p + 1) * blocks, :] for m in range(start, start + tile)],
                    axis=0,
                )
                for p in range(params)
            ],
            axis=1,
        )
        total += jnp.dot(hit, values, preferred_element_type=jnp.float32)
    return total


def same_core():
    core = lax.axis_index("cuts") % CORES
    return [CORES * i + core for i in range(NEAR)]


def sums_kernel(
    offsets_ref, band_ref, radial_ref, wants_ref, all_ref, row_ref, basis_ref, out_ref, turned_ref
):
    for b in range(turned_ref.shape[0]):
        turned_ref[b] = basis_ref[0, b].T
    width = all_ref.shape[2]
    params, bands = band_ref.shape
    near, blocks, _ = out_ref.shape
    count = NEAR * blocks
    patches = all_ref.shape[0] * NEAR * PD
    wanted = jnp.concatenate([column(wants_ref[i : i + 1, :], blocks) for i in range(near)], axis=0)
    beside = patch_sums(wanted, row_ref, params, blocks)
    for p in range(params):
        lanes = slice(p * width, (p + 1) * width)
        radial = beside[:, lanes] * radial_ref[p]
        for i in range(near):
            out_ref[i, :, lanes] = radial[i * blocks : (i + 1) * blocks].astype(out_ref.dtype)
    mine = jnp.concatenate([column(wants_ref[pl.ds(i, 1), :], blocks) for i in same_core()], axis=0)
    wanted = [mine]
    for j in range(bands):
        moved = mine + offsets_ref[j]
        moved = jnp.where(moved < 0, moved + patches, moved)
        wanted.append(jnp.where(moved >= patches, moved - patches, moved))
    total = patch_sums(jnp.concatenate(wanted, axis=0), all_ref, params, blocks)
    core = lax.axis_index("cuts") % CORES
    for p in range(params):
        lanes = slice(p * width, (p + 1) * width)
        part = total[:, lanes]
        centre = part[:count]
        smooth = centre - (2.0 * radial_ref[p]) * centre
        for j in range(bands):
            shifted = part[(j + 1) * count : (j + 2) * count]
            smooth = smooth + band_ref[p, j] * (shifted - centre)
        radial = beside[:, lanes] * radial_ref[p]
        for i in range(NEAR):
            both = [radial[(CORES * i + c) * blocks : (CORES * i + c + 1) * blocks] for c in range(CORES)]
            added = jnp.where(core == 0, both[0], both[1]) + smooth[i * blocks : (i + 1) * blocks]
            out_ref[pl.ds(CORES * i + core, 1), :, lanes] = added[None].astype(out_ref.dtype)


def expand_kernel(parts_ref, turned_ref, valid_ref, out_ref, rows_ref):
    params, _, blocks, points = out_ref.shape
    width = turned_ref.shape[1]
    smooth = sum(parts_ref[i].astype(jnp.float32) for i in range(parts_ref.shape[0]))
    for p in range(params):
        rows_ref[p] = smooth[:, p * width : (p + 1) * width]
    for b in range(blocks):
        picked = rows_ref[:, b, :].astype(jnp.bfloat16)
        rows_ref[:, b, :] = jnp.dot(picked, turned_ref[b], preferred_element_type=jnp.float32)
    inside = inside_mask(valid_ref, blocks, points)
    for p in range(params):
        out_ref[p, 0] = jnp.where(inside, rows_ref[p], 0.0)


VMEM = pl.BlockSpec(memory_space=pltpu.VMEM)
HBM = pl.BlockSpec(memory_space=pltpu.HBM)
SMEM = pl.BlockSpec(memory_space=pltpu.SMEM)


def call(kernel, ins, out_shape, flops, scratch=()):
    many = isinstance(out_shape, tuple)
    return pl.pallas_call(
        kernel,
        out_shape=out_shape,
        in_specs=list(ins),
        out_specs=(VMEM,) * len(out_shape) if many else VMEM,
        scratch_shapes=list(scratch),
        compiler_params=pltpu.CompilerParams(vmem_limit_bytes=24 * 2**20),
        cost_estimate=pl.CostEstimate(flops=flops, bytes_accessed=2**21, transcendentals=0),
    )


def body(
    gradient, basis, block_owner, block_local, valid_count, band_offsets, band_weight, radial_weight
):
    params, _, blocks, points = gradient.shape
    width = basis.shape[3]
    cuts, rows = lax.axis_size("cuts"), lax.axis_size("group")
    chips = cuts // CORES
    values = params * width
    near = NEAR * CORES
    sets = [list(range(first, first + near)) for first in range(0, cuts, near)]
    own = block_owner[:, :, 0] * PD + block_local
    wants = lax.all_gather(own, "cuts", axis_index_groups=sets, tiled=True)
    payload = call(
        project_kernel,
        [HBM] * 2 + [VMEM] * 2,
        jax.ShapeDtypeStruct((params * blocks + ID_ROWS, width), jnp.bfloat16),
        2 * blocks * params * points * width,
        [
            pltpu.VMEM(gradient.shape, gradient.dtype),
            pltpu.VMEM(basis.shape, basis.dtype),
            pltpu.VMEM((params, blocks, width), jnp.float32),
            pltpu.VMEM((ID_ROWS, 128), jnp.int32),
            pltpu.SemaphoreType.DMA((2,)),
        ],
    )(gradient, basis, own, valid_count)
    shares = [
        [CORES * z + c for z in range(first, chips, NEAR) for c in range(CORES)] for first in range(NEAR)
    ]
    gathered = lax.all_gather(payload, "cuts", axis_index_groups=shares)
    pairs = [
        (r * cuts + d, q * cuts + d)
        for r in range(rows)
        for d in range(cuts)
        for q in [r + 1 if d % CORES else r - 1]
        if 0 <= q < rows
    ]
    neighbour = lax.ppermute(gathered, ("group", "cuts"), pairs)
    one_hot = blocks * blocks * cuts * values
    for_near, turned = call(
        sums_kernel,
        [SMEM] * 3 + [VMEM] * 4,
        (
            jax.ShapeDtypeStruct((near, blocks, values), jnp.bfloat16),
            jax.ShapeDtypeStruct((blocks, width, points), basis.dtype),
        ),
        14 * one_hot,
    )(band_offsets, band_weight, radial_weight, wants, gathered, neighbour, basis)
    parts = lax.all_to_all(for_near, "cuts", 0, 0, axis_index_groups=sets, tiled=True)
    return call(
        expand_kernel,
        [VMEM] * 3,
        jax.ShapeDtypeStruct((params, 1, blocks, points), jnp.float32),
        2 * blocks * params * points * width,
        [pltpu.VMEM((params, blocks, width), jnp.float32)],
    )(parts, turned, valid_count)


def solution(mesh):
    return jax.shard_map(
        body,
        mesh=mesh,
        in_specs=(
            P(None, "group", "cuts", None),
            P("group", "cuts", None, None),
            P("group", "cuts", None),
            P("group", "cuts"),
            P("group", "cuts"),
            P(),
            P(),
            P(),
        ),
        out_specs=P(None, "group", "cuts", None),
        check_vma=False,
    )
```

```python
import jax
import jax.numpy as jnp
from jax import lax
from jax.experimental import pallas as pl
from jax.experimental.pallas import tpu as pltpu
from jax.sharding import PartitionSpec as P

PD = 16
CORES = 2
NEAR = 4
ID_ROWS = 8


def column(row, count):
    lanes = row.shape[1]
    wide = jnp.broadcast_to(row, (count, lanes))
    at = lax.broadcasted_iota(jnp.int32, (count, lanes), 0) == lax.broadcasted_iota(
        jnp.int32, (count, lanes), 1
    )
    return jnp.sum(jnp.where(at, wide, 0), axis=1, keepdims=True)


def inside_mask(valid_ref, blocks, points):
    count = column(valid_ref[...], blocks)
    return lax.broadcasted_iota(jnp.int32, (blocks, points), 1) < count


def quarter(position):
    return position // (NEAR * CORES) % 2 * CORES + position % CORES


def project_kernel(
    gradient_hbm, basis_hbm, patch_ref, valid_ref, early_ref, payload_ref, gradient_ref, basis_ref, rows_ref, ids_ref, done
):
    copies = [
        pltpu.make_async_copy(gradient_hbm, gradient_ref, done.at[0]),
        pltpu.make_async_copy(basis_hbm, basis_ref, done.at[1]),
    ]
    for copy in copies:
        copy.start()
    params, _, blocks, points = gradient_ref.shape
    inside = inside_mask(valid_ref, blocks, points)
    ids_ref[...] = jnp.zeros_like(ids_ref)
    ids_ref[0:1, 0:blocks] = patch_ref[0:1, :] // PD
    ids_ref[1:2, 0:blocks] = patch_ref[0:1, :] % PD
    ids = pltpu.roll(ids_ref[...].astype(jnp.float32), quarter(lax.axis_index("cuts")) * blocks, 1)
    payload_ref[params * blocks :, :] = ids.astype(jnp.bfloat16)
    copies[0].wait()
    for p in range(params):
        rows_ref[p] = jnp.where(inside, gradient_ref[p, 0], 0.0)
    copies[1].wait()
    for b in range(blocks):
        masked = rows_ref[:, b, :].astype(jnp.bfloat16)
        rows_ref[:, b, :] = jnp.dot(masked, basis_ref[0, b], preferred_element_type=jnp.float32)
    for p in range(params):
        payload_ref[p * blocks : (p + 1) * blocks, :] = rows_ref[p].astype(jnp.bfloat16)


def patch_sums(wanted, all_ref, params, blocks):
    members, _, width = all_ref.shape
    group = 128 // blocks
    tile = 2 * group
    total = jnp.zeros((wanted.shape[0], params * width), jnp.float32)
    for start in range(0, members, tile):
        ids = []
        for half in range(start, start + tile, group):
            ids.append(
                sum(all_ref[m, params * blocks :, :].astype(jnp.float32) for m in range(half, half + group))
            )
        ids = jnp.concatenate(ids, axis=1)
        patch = (ids[0:1] * PD + ids[1:2]).astype(jnp.int32)
        hit = jnp.where(wanted == patch, 1.0, 0.0).astype(jnp.bfloat16)
        values = jnp.concatenate(
            [
                jnp.concatenate(
                    [all_ref[m, p * blocks : (p + 1) * blocks, :] for m in range(start, start + tile)],
                    axis=0,
                )
                for p in range(params)
            ],
            axis=1,
        )
        total += jnp.dot(hit, values, preferred_element_type=jnp.float32)
    return total


def same_core():
    core = lax.axis_index("cuts") % CORES
    return [CORES * i + core for i in range(NEAR)]


def ids_of(ids, i):
    place, slot = lax.axis_index("cuts"), 0
    for bit in range(3):
        mine = place // (1 << bit) % 2
        other = i // (1 << bit) % 2
        slot = slot + (mine + other - 2 * mine * other) * (1 << bit)
    blocks = ids.shape[1]
    return column(ids[pl.ds(slot, 1), :], blocks)


def lateral_kernel(
    offsets_ref, band_ref, radial_ref, early_ref, late_ref, all_ref, basis_ref, out_ref, turned_ref, ids_ref
):
    for b in range(turned_ref.shape[0]):
        turned_ref[b] = basis_ref[0, b].T
    width = all_ref.shape[2]
    params, bands = band_ref.shape
    _, blocks, _ = out_ref.shape
    count = NEAR * blocks
    patches = all_ref.shape[0] * NEAR * PD
    ids_ref[...] = jnp.maximum(early_ref[...], late_ref[...])
    mine = jnp.concatenate([ids_of(ids_ref, i) for i in same_core()], axis=0)
    wanted = [mine]
    for j in range(bands):
        moved = mine + offsets_ref[j]
        moved = jnp.where(moved < 0, moved + patches, moved)
        wanted.append(jnp.where(moved >= patches, moved - patches, moved))
    total = patch_sums(jnp.concatenate(wanted, axis=0), all_ref, params, blocks)
    out_ref[...] = jnp.zeros_like(out_ref)
    for p in range(params):
        lanes = slice(p * width, (p + 1) * width)
        part = total[:, lanes]
        centre = part[:count]
        smooth = centre - (2.0 * radial_ref[p]) * centre
        for j in range(bands):
            shifted = part[(j + 1) * count : (j + 2) * count]
            smooth = smooth + band_ref[p, j] * (shifted - centre)
        for n, i in enumerate(same_core()):
            out_ref[pl.ds(i, 1), :, lanes] = smooth[None, n * blocks : (n + 1) * blocks]


def radial_kernel(radial_ref, ids_ref, row_ref, part_ref, out_ref):
    width = row_ref.shape[2]
    near, blocks, values = out_ref.shape
    params = values // width
    wanted = jnp.concatenate([ids_of(ids_ref, i) for i in range(near)], axis=0)
    total = patch_sums(wanted, row_ref, params, blocks)
    for p in range(params):
        lanes = slice(p * width, (p + 1) * width)
        radial = total[:, lanes] * radial_ref[p]
        for i in range(near):
            part = part_ref[i, :, lanes] + radial[i * blocks : (i + 1) * blocks]
            out_ref[i, :, lanes] = part.astype(out_ref.dtype)


def expand_kernel(parts_ref, turned_ref, valid_ref, out_ref, rows_ref):
    params, _, blocks, points = out_ref.shape
    width = turned_ref.shape[1]
    smooth = sum(parts_ref[i].astype(jnp.float32) for i in range(parts_ref.shape[0]))
    for p in range(params):
        rows_ref[p] = smooth[:, p * width : (p + 1) * width]
    for b in range(blocks):
        picked = rows_ref[:, b, :].astype(jnp.bfloat16)
        rows_ref[:, b, :] = jnp.dot(picked, turned_ref[b], preferred_element_type=jnp.float32)
    inside = inside_mask(valid_ref, blocks, points)
    for p in range(params):
        out_ref[p, 0] = jnp.where(inside, rows_ref[p], 0.0)


VMEM = pl.BlockSpec(memory_space=pltpu.VMEM)
HBM = pl.BlockSpec(memory_space=pltpu.HBM)
SMEM = pl.BlockSpec(memory_space=pltpu.SMEM)


def call(kernel, ins, out_shape, flops, scratch=()):
    many = isinstance(out_shape, tuple)
    return pl.pallas_call(
        kernel,
        out_shape=out_shape,
        in_specs=list(ins),
        out_specs=(VMEM,) * len(out_shape) if many else VMEM,
        scratch_shapes=list(scratch),
        compiler_params=pltpu.CompilerParams(vmem_limit_bytes=24 * 2**20),
        cost_estimate=pl.CostEstimate(flops=flops, bytes_accessed=2**21, transcendentals=0),
    )


def body(
    gradient, basis, block_owner, block_local, valid_count, band_offsets, band_weight, radial_weight
):
    params, _, blocks, points = gradient.shape
    width = basis.shape[3]
    cuts, rows = lax.axis_size("cuts"), lax.axis_size("group")
    chips = cuts // CORES
    values = params * width
    near = NEAR * CORES
    sets = [list(range(first, first + near)) for first in range(0, cuts, near)]
    own = block_owner[:, :, 0] * PD + block_local

    def wanted_near(own, chosen):
        wants = own
        for bit in range(3):
            pairs = [(d, d ^ (1 << bit)) for d in range(cuts) if d // CORES in chosen]
            wants = jnp.concatenate([wants, lax.ppermute(wants, "cuts", pairs)])
        return wants

    early = wanted_near(own, range(chips // 4))
    payload = call(
        project_kernel,
        [HBM] * 2 + [VMEM] * 3,
        jax.ShapeDtypeStruct((params * blocks + ID_ROWS, width), jnp.bfloat16),
        2 * blocks * params * points * width,
        [
            pltpu.VMEM(gradient.shape, gradient.dtype),
            pltpu.VMEM(basis.shape, basis.dtype),
            pltpu.VMEM((params, blocks, width), jnp.float32),
            pltpu.VMEM((ID_ROWS, 128), jnp.int32),
            pltpu.SemaphoreType.DMA((2,)),
        ],
    )(gradient, basis, own, valid_count, early)
    shares = [
        [CORES * z + c for z in range(first, chips, NEAR) for c in range(CORES)] for first in range(NEAR)
    ]
    gathered = lax.all_gather(payload, "cuts", axis_index_groups=shares)
    pairs = [
        (r * cuts + d, q * cuts + d)
        for r in range(rows)
        for d in range(cuts)
        for q in [r + 1 if d % CORES else r - 1]
        if 0 <= q < rows
    ]
    neighbour = lax.ppermute(gathered, ("group", "cuts"), pairs)
    position = lax.axis_index("cuts")
    place = (position // (NEAR * CORES) * CORES + position % CORES, params * blocks, quarter(position) * blocks)
    ids = lax.dynamic_slice(gathered, place, (1, 2, blocks))[0].astype(jnp.int32)
    late = wanted_near(ids[0:1] * PD + ids[1:2], range(chips // 4, chips))
    one_hot = blocks * blocks * cuts * values
    part, turned, wants = call(
        lateral_kernel,
        [SMEM] * 3 + [VMEM] * 4,
        (
            jax.ShapeDtypeStruct((near, blocks, values), jnp.float32),
            jax.ShapeDtypeStruct((blocks, width, points), basis.dtype),
            jax.ShapeDtypeStruct((near, blocks), jnp.int32),
        ),
        10 * one_hot,
    )(band_offsets, band_weight, radial_weight, early, late, gathered, basis)
    for_near = call(
        radial_kernel,
        [SMEM] + [VMEM] * 3,
        jax.ShapeDtypeStruct((near, blocks, values), jnp.bfloat16),
        4 * one_hot,
    )(radial_weight, wants, neighbour, part)
    parts = lax.all_to_all(for_near, "cuts", 0, 0, axis_index_groups=sets, tiled=True)
    return call(
        expand_kernel,
        [VMEM] * 3,
        jax.ShapeDtypeStruct((params, 1, blocks, points), jnp.float32),
        2 * blocks * params * points * width,
        [pltpu.VMEM((params, blocks, width), jnp.float32)],
    )(parts, turned, valid_count)


def solution(mesh):
    return jax.shard_map(
        body,
        mesh=mesh,
        in_specs=(
            P(None, "group", "cuts", None),
            P("group", "cuts", None, None),
            P("group", "cuts", None),
            P("group", "cuts"),
            P("group", "cuts"),
            P(),
            P(),
            P(),
        ),
        out_specs=P(None, "group", "cuts", None),
        check_vma=False,
    )
```

```python
import jax
import jax.numpy as jnp
from jax import lax
from jax.experimental import pallas as pl
from jax.experimental.pallas import tpu as pltpu
from jax.sharding import PartitionSpec as P

PD = 16
CORES = 2
NEAR = 4
ID_ROWS = 8


def column(row, count):
    lanes = row.shape[1]
    wide = jnp.broadcast_to(row, (count, lanes))
    at = lax.broadcasted_iota(jnp.int32, (count, lanes), 0) == lax.broadcasted_iota(
        jnp.int32, (count, lanes), 1
    )
    return jnp.sum(jnp.where(at, wide, 0), axis=1, keepdims=True)


def inside_mask(valid_ref, blocks, points):
    count = column(valid_ref[...], blocks)
    return lax.broadcasted_iota(jnp.int32, (blocks, points), 1) < count


def project_kernel(
    gradient_hbm, basis_hbm, patch_ref, valid_ref, payload_ref, gradient_ref, basis_ref, rows_ref, ids_ref, done
):
    copies = [
        pltpu.make_async_copy(gradient_hbm, gradient_ref, done.at[0]),
        pltpu.make_async_copy(basis_hbm, basis_ref, done.at[1]),
    ]
    for copy in copies:
        copy.start()
    params, _, blocks, points = gradient_ref.shape
    inside = inside_mask(valid_ref, blocks, points)
    ids_ref[...] = jnp.zeros_like(ids_ref)
    ids_ref[0:1, 0:blocks] = patch_ref[0:1, :] // PD
    ids_ref[1:2, 0:blocks] = patch_ref[0:1, :] % PD
    position = lax.axis_index("cuts")
    quarter = (position // (NEAR * CORES)) % 2 * CORES + position % CORES
    ids = pltpu.roll(ids_ref[...].astype(jnp.float32), quarter * blocks, 1)
    payload_ref[params * blocks :, :] = ids.astype(jnp.bfloat16)
    copies[0].wait()
    for p in range(params):
        rows_ref[p] = jnp.where(inside, gradient_ref[p, 0], 0.0)
    copies[1].wait()
    for b in range(blocks):
        masked = rows_ref[:, b, :].astype(jnp.bfloat16)
        rows_ref[:, b, :] = jnp.dot(masked, basis_ref[0, b], preferred_element_type=jnp.float32)
    for p in range(params):
        payload_ref[p * blocks : (p + 1) * blocks, :] = rows_ref[p].astype(jnp.bfloat16)


def patch_sums(wanted, all_ref, params, blocks):
    members, _, width = all_ref.shape
    group = 128 // blocks
    tile = 2 * group
    total = jnp.zeros((wanted.shape[0], params * width), jnp.float32)
    for start in range(0, members, tile):
        ids = []
        for half in range(start, start + tile, group):
            ids.append(
                sum(all_ref[m, params * blocks :, :].astype(jnp.float32) for m in range(half, half + group))
            )
        ids = jnp.concatenate(ids, axis=1)
        patch = (ids[0:1] * PD + ids[1:2]).astype(jnp.int32)
        hit = jnp.where(wanted == patch, 1.0, 0.0).astype(jnp.bfloat16)
        values = jnp.concatenate(
            [
                jnp.concatenate(
                    [all_ref[m, p * blocks : (p + 1) * blocks, :] for m in range(start, start + tile)],
                    axis=0,
                )
                for p in range(params)
            ],
            axis=1,
        )
        total += jnp.dot(hit, values, preferred_element_type=jnp.float32)
    return total


def same_core():
    core = lax.axis_index("cuts") % CORES
    return [CORES * i + core for i in range(NEAR)]


def sums_kernel(
    offsets_ref, band_ref, radial_ref, wants_ref, all_ref, row_ref, basis_ref, out_ref, turned_ref
):
    for b in range(turned_ref.shape[0]):
        turned_ref[b] = basis_ref[0, b].T
    width = all_ref.shape[2]
    params, bands = band_ref.shape
    near, blocks, _ = out_ref.shape
    count = NEAR * blocks
    patches = all_ref.shape[0] * NEAR * PD
    wanted = jnp.concatenate([column(wants_ref[i : i + 1, :], blocks) for i in range(near)], axis=0)
    beside = patch_sums(wanted, row_ref, params, blocks)
    for p in range(params):
        lanes = slice(p * width, (p + 1) * width)
        radial = beside[:, lanes] * radial_ref[p]
        for i in range(near):
            out_ref[i, :, lanes] = radial[i * blocks : (i + 1) * blocks].astype(out_ref.dtype)
    mine = jnp.concatenate([column(wants_ref[pl.ds(i, 1), :], blocks) for i in same_core()], axis=0)
    wanted = [mine]
    for j in range(bands):
        moved = mine + offsets_ref[j]
        moved = jnp.where(moved < 0, moved + patches, moved)
        wanted.append(jnp.where(moved >= patches, moved - patches, moved))
    total = patch_sums(jnp.concatenate(wanted, axis=0), all_ref, params, blocks)
    core = lax.axis_index("cuts") % CORES
    for p in range(params):
        lanes = slice(p * width, (p + 1) * width)
        part = total[:, lanes]
        centre = part[:count]
        smooth = centre - (2.0 * radial_ref[p]) * centre
        for j in range(bands):
            shifted = part[(j + 1) * count : (j + 2) * count]
            smooth = smooth + band_ref[p, j] * (shifted - centre)
        radial = beside[:, lanes] * radial_ref[p]
        for i in range(NEAR):
            both = [radial[(CORES * i + c) * blocks : (CORES * i + c + 1) * blocks] for c in range(CORES)]
            added = jnp.where(core == 0, both[0], both[1]) + smooth[i * blocks : (i + 1) * blocks]
            out_ref[pl.ds(CORES * i + core, 1), :, lanes] = added[None].astype(out_ref.dtype)


def expand_kernel(parts_ref, turned_ref, valid_ref, out_ref, rows_ref):
    params, _, blocks, points = out_ref.shape
    width = turned_ref.shape[1]
    smooth = sum(parts_ref[i].astype(jnp.float32) for i in range(parts_ref.shape[0]))
    for p in range(params):
        rows_ref[p] = smooth[:, p * width : (p + 1) * width]
    for b in range(blocks):
        picked = rows_ref[:, b, :].astype(jnp.bfloat16)
        rows_ref[:, b, :] = jnp.dot(picked, turned_ref[b], preferred_element_type=jnp.float32)
    inside = inside_mask(valid_ref, blocks, points)
    for p in range(params):
        out_ref[p, 0] = jnp.where(inside, rows_ref[p], 0.0)


VMEM = pl.BlockSpec(memory_space=pltpu.VMEM)
HBM = pl.BlockSpec(memory_space=pltpu.HBM)
SMEM = pl.BlockSpec(memory_space=pltpu.SMEM)


def call(kernel, ins, out_shape, flops, scratch=()):
    many = isinstance(out_shape, tuple)
    return pl.pallas_call(
        kernel,
        out_shape=out_shape,
        in_specs=list(ins),
        out_specs=(VMEM,) * len(out_shape) if many else VMEM,
        scratch_shapes=list(scratch),
        compiler_params=pltpu.CompilerParams(vmem_limit_bytes=24 * 2**20),
        cost_estimate=pl.CostEstimate(flops=flops, bytes_accessed=2**21, transcendentals=0),
    )


def body(
    gradient, basis, block_owner, block_local, valid_count, band_offsets, band_weight, radial_weight
):
    params, _, blocks, points = gradient.shape
    width = basis.shape[3]
    cuts, rows = lax.axis_size("cuts"), lax.axis_size("group")
    chips = cuts // CORES
    values = params * width
    near = NEAR * CORES
    sets = [list(range(first, first + near)) for first in range(0, cuts, near)]
    own = block_owner[:, :, 0] * PD + block_local
    payload = call(
        project_kernel,
        [HBM] * 2 + [VMEM] * 2,
        jax.ShapeDtypeStruct((params * blocks + ID_ROWS, width), jnp.bfloat16),
        2 * blocks * params * points * width,
        [
            pltpu.VMEM(gradient.shape, gradient.dtype),
            pltpu.VMEM(basis.shape, basis.dtype),
            pltpu.VMEM((params, blocks, width), jnp.float32),
            pltpu.VMEM((ID_ROWS, 128), jnp.int32),
            pltpu.SemaphoreType.DMA((2,)),
        ],
    )(gradient, basis, own, valid_count)
    shares = [
        [CORES * z + c for z in range(first, chips, NEAR) for c in range(CORES)] for first in range(NEAR)
    ]
    gathered = lax.all_gather(payload, "cuts", axis_index_groups=shares)
    pairs = [
        (r * cuts + d, q * cuts + d)
        for r in range(rows)
        for d in range(cuts)
        for q in [r + 1 if d % CORES else r - 1]
        if 0 <= q < rows
    ]
    neighbour = lax.ppermute(gathered, ("group", "cuts"), pairs)
    position = lax.axis_index("cuts")
    member, lane = position // (NEAR * CORES) * CORES, position // (NEAR * CORES) % 2 * CORES
    ids = [
        lax.dynamic_slice(
            gathered, (member + c, params * blocks, (lane + c) * blocks), (1, 2, blocks)
        )[0].astype(jnp.int32)
        for c in range(CORES)
    ]
    ids = jnp.concatenate([each[0:1] * PD + each[1:2] for each in ids])
    lines = [[at + CORES * i + c for i in range(NEAR)] for at in range(0, cuts, near) for c in range(CORES)]
    wants = lax.all_gather(ids, "cuts", axis_index_groups=lines, tiled=True)
    one_hot = blocks * blocks * cuts * values
    for_near, turned = call(
        sums_kernel,
        [SMEM] * 3 + [VMEM] * 4,
        (
            jax.ShapeDtypeStruct((near, blocks, values), jnp.bfloat16),
            jax.ShapeDtypeStruct((blocks, width, points), basis.dtype),
        ),
        14 * one_hot,
    )(band_offsets, band_weight, radial_weight, wants, gathered, neighbour, basis)
    parts = lax.all_to_all(for_near, "cuts", 0, 0, axis_index_groups=sets, tiled=True)
    return call(
        expand_kernel,
        [VMEM] * 3,
        jax.ShapeDtypeStruct((params, 1, blocks, points), jnp.float32),
        2 * blocks * params * points * width,
        [pltpu.VMEM((params, blocks, width), jnp.float32)],
    )(parts, turned, valid_count)


def solution(mesh):
    return jax.shard_map(
        body,
        mesh=mesh,
        in_specs=(
            P(None, "group", "cuts", None),
            P("group", "cuts", None, None),
            P("group", "cuts", None),
            P("group", "cuts"),
            P("group", "cuts"),
            P(),
            P(),
            P(),
        ),
        out_specs=P(None, "group", "cuts", None),
        check_vma=False,
    )
```

```python
import jax
import jax.numpy as jnp
from jax import lax
from jax.experimental import pallas as pl
from jax.experimental.pallas import tpu as pltpu
from jax.sharding import PartitionSpec as P

PD = 16
CORES = 2
NEAR = 4
ID_ROWS = 16


def column(row, count):
    lanes = row.shape[1]
    wide = jnp.broadcast_to(row, (count, lanes))
    at = lax.broadcasted_iota(jnp.int32, (count, lanes), 0) == lax.broadcasted_iota(
        jnp.int32, (count, lanes), 1
    )
    return jnp.sum(jnp.where(at, wide, 0), axis=1, keepdims=True)


def inside_mask(valid_ref, blocks, points):
    count = column(valid_ref[...], blocks)
    return lax.broadcasted_iota(jnp.int32, (blocks, points), 1) < count


def project_kernel(
    gradient_hbm, basis_hbm, patch_ref, valid_ref, payload_ref, gradient_ref, basis_ref, rows_ref, ids_ref, done
):
    copies = [
        pltpu.make_async_copy(gradient_hbm, gradient_ref, done.at[0]),
        pltpu.make_async_copy(basis_hbm, basis_ref, done.at[1]),
    ]
    for copy in copies:
        copy.start()
    params, _, blocks, points = gradient_ref.shape
    inside = inside_mask(valid_ref, blocks, points)
    ids_ref[...] = jnp.zeros_like(ids_ref)
    ids_ref[0:1, 0:blocks] = patch_ref[0:1, :] // PD
    ids_ref[1:2, 0:blocks] = patch_ref[0:1, :] % PD
    position = lax.axis_index("cuts")
    quarter = (position // (NEAR * CORES)) % 2 * CORES + position % CORES
    ids = pltpu.roll(ids_ref[...].astype(jnp.float32), quarter * blocks, 1)
    payload_ref[params * blocks :, :] = ids.astype(jnp.bfloat16)
    copies[0].wait()
    for p in range(params):
        rows_ref[p] = jnp.where(inside, gradient_ref[p, 0], 0.0)
    copies[1].wait()
    for b in range(blocks):
        masked = rows_ref[:, b, :].astype(jnp.bfloat16)
        rows_ref[:, b, :] = jnp.dot(masked, basis_ref[0, b], preferred_element_type=jnp.float32)
    for p in range(params):
        payload_ref[p * blocks : (p + 1) * blocks, :] = rows_ref[p].astype(jnp.bfloat16)


def patch_sums(wanted, all_ref, params, blocks):
    members, _, width = all_ref.shape
    group = 128 // blocks
    tile = 2 * group
    total = jnp.zeros((wanted.shape[0], params * width), jnp.float32)
    for start in range(0, members, tile):
        ids = []
        for half in range(start, start + tile, group):
            ids.append(
                sum(all_ref[m, params * blocks :, :].astype(jnp.float32) for m in range(half, half + group))
            )
        ids = jnp.concatenate(ids, axis=1)
        patch = (ids[0:1] * PD + ids[1:2]).astype(jnp.int32)
        hit = jnp.where(wanted == patch, 1.0, 0.0).astype(jnp.bfloat16)
        values = jnp.concatenate(
            [
                jnp.concatenate(
                    [all_ref[m, p * blocks : (p + 1) * blocks, :] for m in range(start, start + tile)],
                    axis=0,
                )
                for p in range(params)
            ],
            axis=1,
        )
        total += jnp.dot(hit, values, preferred_element_type=jnp.float32)
    return total


def same_core():
    core = lax.axis_index("cuts") % CORES
    return [CORES * i + core for i in range(NEAR)]


def sums_kernel(
    offsets_ref, band_ref, radial_ref, wants_ref, all_ref, row_ref, basis_ref, out_ref, turned_ref
):
    for b in range(turned_ref.shape[0]):
        turned_ref[b] = basis_ref[0, b].T
    width = all_ref.shape[2]
    params, bands = band_ref.shape
    near, blocks, _ = out_ref.shape
    count = NEAR * blocks
    patches = all_ref.shape[0] * NEAR * PD
    wanted = jnp.concatenate([column(wants_ref[i : i + 1, :], blocks) for i in range(near)], axis=0)
    beside = patch_sums(wanted, row_ref, params, blocks)
    for p in range(params):
        lanes = slice(p * width, (p + 1) * width)
        radial = beside[:, lanes] * radial_ref[p]
        for i in range(near):
            out_ref[i, :, lanes] = radial[i * blocks : (i + 1) * blocks].astype(out_ref.dtype)
    mine = jnp.concatenate([column(wants_ref[pl.ds(i, 1), :], blocks) for i in same_core()], axis=0)
    wanted = [mine]
    for j in range(bands):
        moved = mine + offsets_ref[j]
        moved = jnp.where(moved < 0, moved + patches, moved)
        wanted.append(jnp.where(moved >= patches, moved - patches, moved))
    total = patch_sums(jnp.concatenate(wanted, axis=0), all_ref, params, blocks)
    core = lax.axis_index("cuts") % CORES
    for p in range(params):
        lanes = slice(p * width, (p + 1) * width)
        part = total[:, lanes]
        centre = part[:count]
        smooth = centre - (2.0 * radial_ref[p]) * centre
        for j in range(bands):
            shifted = part[(j + 1) * count : (j + 2) * count]
            smooth = smooth + band_ref[p, j] * (shifted - centre)
        radial = beside[:, lanes] * radial_ref[p]
        for i in range(NEAR):
            both = [radial[(CORES * i + c) * blocks : (CORES * i + c + 1) * blocks] for c in range(CORES)]
            added = jnp.where(core == 0, both[0], both[1]) + smooth[i * blocks : (i + 1) * blocks]
            out_ref[pl.ds(CORES * i + core, 1), :, lanes] = added[None].astype(out_ref.dtype)


def expand_kernel(parts_ref, turned_ref, valid_ref, out_ref, rows_ref):
    params, _, blocks, points = out_ref.shape
    width = turned_ref.shape[1]
    smooth = sum(parts_ref[i].astype(jnp.float32) for i in range(parts_ref.shape[0]))
    for p in range(params):
        rows_ref[p] = smooth[:, p * width : (p + 1) * width]
    for b in range(blocks):
        picked = rows_ref[:, b, :].astype(jnp.bfloat16)
        rows_ref[:, b, :] = jnp.dot(picked, turned_ref[b], preferred_element_type=jnp.float32)
    inside = inside_mask(valid_ref, blocks, points)
    for p in range(params):
        out_ref[p, 0] = jnp.where(inside, rows_ref[p], 0.0)


VMEM = pl.BlockSpec(memory_space=pltpu.VMEM)
HBM = pl.BlockSpec(memory_space=pltpu.HBM)
SMEM = pl.BlockSpec(memory_space=pltpu.SMEM)


def call(kernel, ins, out_shape, flops, scratch=()):
    many = isinstance(out_shape, tuple)
    return pl.pallas_call(
        kernel,
        out_shape=out_shape,
        in_specs=list(ins),
        out_specs=(VMEM,) * len(out_shape) if many else VMEM,
        scratch_shapes=list(scratch),
        compiler_params=pltpu.CompilerParams(vmem_limit_bytes=24 * 2**20),
        cost_estimate=pl.CostEstimate(flops=flops, bytes_accessed=2**21, transcendentals=0),
    )


def body(
    gradient, basis, block_owner, block_local, valid_count, band_offsets, band_weight, radial_weight
):
    params, _, blocks, points = gradient.shape
    width = basis.shape[3]
    cuts, rows = lax.axis_size("cuts"), lax.axis_size("group")
    chips = cuts // CORES
    values = params * width
    near = NEAR * CORES
    sets = [list(range(first, first + near)) for first in range(0, cuts, near)]
    own = block_owner[:, :, 0] * PD + block_local
    payload = call(
        project_kernel,
        [HBM] * 2 + [VMEM] * 2,
        jax.ShapeDtypeStruct((params * blocks + ID_ROWS, width), jnp.bfloat16),
        2 * blocks * params * points * width,
        [
            pltpu.VMEM(gradient.shape, gradient.dtype),
            pltpu.VMEM(basis.shape, basis.dtype),
            pltpu.VMEM((params, blocks, width), jnp.float32),
            pltpu.VMEM((ID_ROWS, 128), jnp.int32),
            pltpu.SemaphoreType.DMA((2,)),
        ],
    )(gradient, basis, own, valid_count)
    shares = [
        [CORES * z + c for z in range(first, chips, NEAR) for c in range(CORES)] for first in range(NEAR)
    ]
    gathered = lax.all_gather(payload, "cuts", axis_index_groups=shares)
    pairs = [
        (r * cuts + d, q * cuts + d)
        for r in range(rows)
        for d in range(cuts)
        for q in [r + 1 if d % CORES else r - 1]
        if 0 <= q < rows
    ]
    neighbour = lax.ppermute(gathered, ("group", "cuts"), pairs)
    position = lax.axis_index("cuts")
    member, lane = position // (NEAR * CORES) * CORES, position // (NEAR * CORES) % 2 * CORES
    ids = [
        lax.dynamic_slice(
            gathered, (member + c, params * blocks, (lane + c) * blocks), (1, 2, blocks)
        )[0].astype(jnp.int32)
        for c in range(CORES)
    ]
    ids = jnp.concatenate([each[0:1] * PD + each[1:2] for each in ids])
    lines = [[at + CORES * i + c for i in range(NEAR)] for at in range(0, cuts, near) for c in range(CORES)]
    wants = lax.all_gather(ids, "cuts", axis_index_groups=lines, tiled=True)
    one_hot = blocks * blocks * cuts * values
    for_near, turned = call(
        sums_kernel,
        [SMEM] * 3 + [VMEM] * 4,
        (
            jax.ShapeDtypeStruct((near, blocks, values), jnp.bfloat16),
            jax.ShapeDtypeStruct((blocks, width, points), basis.dtype),
        ),
        14 * one_hot,
    )(band_offsets, band_weight, radial_weight, wants, gathered, neighbour, basis)
    parts = lax.all_to_all(for_near, "cuts", 0, 0, axis_index_groups=sets, tiled=True)
    return call(
        expand_kernel,
        [VMEM] * 3,
        jax.ShapeDtypeStruct((params, 1, blocks, points), jnp.float32),
        2 * blocks * params * points * width,
        [pltpu.VMEM((params, blocks, width), jnp.float32)],
    )(parts, turned, valid_count)


def solution(mesh):
    return jax.shard_map(
        body,
        mesh=mesh,
        in_specs=(
            P(None, "group", "cuts", None),
            P("group", "cuts", None, None),
            P("group", "cuts", None),
            P("group", "cuts"),
            P("group", "cuts"),
            P(),
            P(),
            P(),
        ),
        out_specs=P(None, "group", "cuts", None),
        check_vma=False,
    )
```

```python
import jax
import jax.numpy as jnp
from jax import lax
from jax.experimental import pallas as pl
from jax.experimental.pallas import tpu as pltpu
from jax.sharding import PartitionSpec as P

PD = 16
CORES = 2
NEAR = 4
ID_ROWS = 16


def column(row, count):
    lanes = row.shape[1]
    wide = jnp.broadcast_to(row, (count, lanes))
    at = lax.broadcasted_iota(jnp.int32, (count, lanes), 0) == lax.broadcasted_iota(
        jnp.int32, (count, lanes), 1
    )
    return jnp.sum(jnp.where(at, wide, 0), axis=1, keepdims=True)


def inside_mask(valid_ref, blocks, points):
    count = column(valid_ref[...], blocks)
    return lax.broadcasted_iota(jnp.int32, (blocks, points), 1) < count


def project_kernel(
    gradient_hbm, basis_hbm, patch_ref, valid_ref, offsets_ref, payload_ref, shifts_ref, gradient_ref, basis_ref, rows_ref, ids_ref, done
):
    copies = [
        pltpu.make_async_copy(gradient_hbm, gradient_ref, done.at[0]),
        pltpu.make_async_copy(basis_hbm, basis_ref, done.at[1]),
    ]
    for copy in copies:
        copy.start()
    params, _, blocks, points = gradient_ref.shape
    inside = inside_mask(valid_ref, blocks, points)
    for j in range(offsets_ref.shape[0]):
        shifts_ref[j : j + 1, :] = jnp.full((1, 128), offsets_ref[j], jnp.int32)
    ids_ref[...] = jnp.zeros_like(ids_ref)
    ids_ref[0:1, 0:blocks] = patch_ref[0:1, :] // PD
    ids_ref[1:2, 0:blocks] = patch_ref[0:1, :] % PD
    position = lax.axis_index("cuts")
    quarter = (position // (NEAR * CORES)) % 2 * CORES + position % CORES
    ids = pltpu.roll(ids_ref[...].astype(jnp.float32), quarter * blocks, 1)
    payload_ref[params * blocks :, :] = ids.astype(jnp.bfloat16)
    copies[0].wait()
    for p in range(params):
        rows_ref[p] = jnp.where(inside, gradient_ref[p, 0], 0.0)
    copies[1].wait()
    for b in range(blocks):
        masked = rows_ref[:, b, :].astype(jnp.bfloat16)
        rows_ref[:, b, :] = jnp.dot(masked, basis_ref[0, b], preferred_element_type=jnp.float32)
    for p in range(params):
        payload_ref[p * blocks : (p + 1) * blocks, :] = rows_ref[p].astype(jnp.bfloat16)


def patch_sums(wanted, all_ref, params, blocks):
    members, _, width = all_ref.shape
    group = 128 // blocks
    tile = 2 * group
    total = jnp.zeros((wanted.shape[0], params * width), jnp.float32)
    for start in range(0, members, tile):
        ids = []
        for half in range(start, start + tile, group):
            ids.append(
                sum(all_ref[m, params * blocks :, :].astype(jnp.float32) for m in range(half, half + group))
            )
        ids = jnp.concatenate(ids, axis=1)
        patch = (ids[0:1] * PD + ids[1:2]).astype(jnp.int32)
        hit = jnp.where(wanted == patch, 1.0, 0.0).astype(jnp.bfloat16)
        values = jnp.concatenate(
            [
                jnp.concatenate(
                    [all_ref[m, p * blocks : (p + 1) * blocks, :] for m in range(start, start + tile)],
                    axis=0,
                )
                for p in range(params)
            ],
            axis=1,
        )
        total += jnp.dot(hit, values, preferred_element_type=jnp.float32)
    return total


def same_core():
    core = lax.axis_index("cuts") % CORES
    return [CORES * i + core for i in range(NEAR)]


def sums_kernel(
    shifts_ref, band_ref, radial_ref, wants_ref, all_ref, row_ref, basis_ref, out_ref, turned_ref
):
    for b in range(turned_ref.shape[0]):
        turned_ref[b] = basis_ref[0, b].T
    width = all_ref.shape[2]
    params, bands = band_ref.shape
    near, blocks, _ = out_ref.shape
    count = NEAR * blocks
    patches = all_ref.shape[0] * NEAR * PD
    wanted = jnp.concatenate([column(wants_ref[i : i + 1, :], blocks) for i in range(near)], axis=0)
    beside = patch_sums(wanted, row_ref, params, blocks)
    for p in range(params):
        lanes = slice(p * width, (p + 1) * width)
        radial = beside[:, lanes] * radial_ref[p]
        for i in range(near):
            out_ref[i, :, lanes] = radial[i * blocks : (i + 1) * blocks].astype(out_ref.dtype)
    mine = jnp.concatenate([column(wants_ref[pl.ds(i, 1), :], blocks) for i in same_core()], axis=0)
    wanted = [mine]
    for j in range(bands):
        moved = mine + shifts_ref[j : j + 1, 0:1]
        moved = jnp.where(moved < 0, moved + patches, moved)
        wanted.append(jnp.where(moved >= patches, moved - patches, moved))
    total = patch_sums(jnp.concatenate(wanted, axis=0), all_ref, params, blocks)
    core = lax.axis_index("cuts") % CORES
    for p in range(params):
        lanes = slice(p * width, (p + 1) * width)
        part = total[:, lanes]
        centre = part[:count]
        smooth = centre - (2.0 * radial_ref[p]) * centre
        for j in range(bands):
            shifted = part[(j + 1) * count : (j + 2) * count]
            smooth = smooth + band_ref[p, j] * (shifted - centre)
        radial = beside[:, lanes] * radial_ref[p]
        for i in range(NEAR):
            both = [radial[(CORES * i + c) * blocks : (CORES * i + c + 1) * blocks] for c in range(CORES)]
            added = jnp.where(core == 0, both[0], both[1]) + smooth[i * blocks : (i + 1) * blocks]
            out_ref[pl.ds(CORES * i + core, 1), :, lanes] = added[None].astype(out_ref.dtype)


def expand_kernel(parts_ref, turned_ref, valid_ref, out_ref, rows_ref):
    params, _, blocks, points = out_ref.shape
    width = turned_ref.shape[1]
    smooth = sum(parts_ref[i].astype(jnp.float32) for i in range(parts_ref.shape[0]))
    for p in range(params):
        rows_ref[p] = smooth[:, p * width : (p + 1) * width]
    for b in range(blocks):
        picked = rows_ref[:, b, :].astype(jnp.bfloat16)
        rows_ref[:, b, :] = jnp.dot(picked, turned_ref[b], preferred_element_type=jnp.float32)
    inside = inside_mask(valid_ref, blocks, points)
    for p in range(params):
        out_ref[p, 0] = jnp.where(inside, rows_ref[p], 0.0)


VMEM = pl.BlockSpec(memory_space=pltpu.VMEM)
HBM = pl.BlockSpec(memory_space=pltpu.HBM)
SMEM = pl.BlockSpec(memory_space=pltpu.SMEM)


def call(kernel, ins, out_shape, flops, scratch=()):
    many = isinstance(out_shape, tuple)
    return pl.pallas_call(
        kernel,
        out_shape=out_shape,
        in_specs=list(ins),
        out_specs=(VMEM,) * len(out_shape) if many else VMEM,
        scratch_shapes=list(scratch),
        compiler_params=pltpu.CompilerParams(vmem_limit_bytes=24 * 2**20),
        cost_estimate=pl.CostEstimate(flops=flops, bytes_accessed=2**21, transcendentals=0),
    )


def body(
    gradient, basis, block_owner, block_local, valid_count, band_offsets, band_weight, radial_weight
):
    params, _, blocks, points = gradient.shape
    width = basis.shape[3]
    cuts, rows = lax.axis_size("cuts"), lax.axis_size("group")
    chips = cuts // CORES
    values = params * width
    near = NEAR * CORES
    sets = [list(range(first, first + near)) for first in range(0, cuts, near)]
    own = block_owner[:, :, 0] * PD + block_local
    payload, shifts = call(
        project_kernel,
        [HBM] * 2 + [VMEM] * 2 + [SMEM],
        (
            jax.ShapeDtypeStruct((params * blocks + ID_ROWS, width), jnp.bfloat16),
            jax.ShapeDtypeStruct((band_offsets.shape[0], 128), jnp.int32),
        ),
        2 * blocks * params * points * width,
        [
            pltpu.VMEM(gradient.shape, gradient.dtype),
            pltpu.VMEM(basis.shape, basis.dtype),
            pltpu.VMEM((params, blocks, width), jnp.float32),
            pltpu.VMEM((ID_ROWS, 128), jnp.int32),
            pltpu.SemaphoreType.DMA((2,)),
        ],
    )(gradient, basis, own, valid_count, band_offsets)
    shares = [
        [CORES * z + c for z in range(first, chips, NEAR) for c in range(CORES)] for first in range(NEAR)
    ]
    gathered = lax.all_gather(payload, "cuts", axis_index_groups=shares)
    pairs = [
        (r * cuts + d, q * cuts + d)
        for r in range(rows)
        for d in range(cuts)
        for q in [r + 1 if d % CORES else r - 1]
        if 0 <= q < rows
    ]
    neighbour = lax.ppermute(gathered, ("group", "cuts"), pairs)
    position = lax.axis_index("cuts")
    member, lane = position // (NEAR * CORES) * CORES, position // (NEAR * CORES) % 2 * CORES
    ids = [
        lax.dynamic_slice(
            gathered, (member + c, params * blocks, (lane + c) * blocks), (1, 2, blocks)
        )[0].astype(jnp.int32)
        for c in range(CORES)
    ]
    ids = jnp.concatenate([each[0:1] * PD + each[1:2] for each in ids])
    lines = [[at + CORES * i + c for i in range(NEAR)] for at in range(0, cuts, near) for c in range(CORES)]
    wants = lax.all_gather(ids, "cuts", axis_index_groups=lines, tiled=True)
    one_hot = blocks * blocks * cuts * values
    for_near, turned = call(
        sums_kernel,
        [VMEM] + [SMEM] * 2 + [VMEM] * 4,
        (
            jax.ShapeDtypeStruct((near, blocks, values), jnp.bfloat16),
            jax.ShapeDtypeStruct((blocks, width, points), basis.dtype),
        ),
        14 * one_hot,
    )(shifts, band_weight, radial_weight, wants, gathered, neighbour, basis)
    parts = lax.all_to_all(for_near, "cuts", 0, 0, axis_index_groups=sets, tiled=True)
    return call(
        expand_kernel,
        [VMEM] * 3,
        jax.ShapeDtypeStruct((params, 1, blocks, points), jnp.float32),
        2 * blocks * params * points * width,
        [pltpu.VMEM((params, blocks, width), jnp.float32)],
    )(parts, turned, valid_count)


def solution(mesh):
    return jax.shard_map(
        body,
        mesh=mesh,
        in_specs=(
            P(None, "group", "cuts", None),
            P("group", "cuts", None, None),
            P("group", "cuts", None),
            P("group", "cuts"),
            P("group", "cuts"),
            P(),
            P(),
            P(),
        ),
        out_specs=P(None, "group", "cuts", None),
        check_vma=False,
    )
```

```python
import jax
import jax.numpy as jnp
from jax import lax
from jax.experimental import pallas as pl
from jax.experimental.pallas import tpu as pltpu
from jax.sharding import PartitionSpec as P

PD = 16
CORES = 2
NEAR = 4
ID_ROWS = 16


def column(row, count):
    lanes = row.shape[1]
    wide = jnp.broadcast_to(row, (count, lanes))
    at = lax.broadcasted_iota(jnp.int32, (count, lanes), 0) == lax.broadcasted_iota(
        jnp.int32, (count, lanes), 1
    )
    return jnp.sum(jnp.where(at, wide, 0), axis=1, keepdims=True)


def inside_mask(valid_ref, blocks, points):
    count = column(valid_ref[...], blocks)
    return lax.broadcasted_iota(jnp.int32, (blocks, points), 1) < count


def project_kernel(
    gradient_hbm, basis_hbm, patch_ref, valid_ref, payload_ref, gradient_ref, basis_ref, rows_ref, ids_ref, done
):
    copies = [
        pltpu.make_async_copy(gradient_hbm, gradient_ref, done.at[0]),
        pltpu.make_async_copy(basis_hbm, basis_ref, done.at[1]),
    ]
    for copy in copies:
        copy.start()
    params, _, blocks, points = gradient_ref.shape
    inside = inside_mask(valid_ref, blocks, points)
    ids_ref[...] = jnp.zeros_like(ids_ref)
    ids_ref[0:1, 0:blocks] = patch_ref[0:1, :] // PD
    ids_ref[1:2, 0:blocks] = patch_ref[0:1, :] % PD
    position = lax.axis_index("cuts")
    quarter = (position // (NEAR * CORES)) % 2 * CORES + position % CORES
    ids = pltpu.roll(ids_ref[...].astype(jnp.float32), quarter * blocks, 1)
    payload_ref[params * blocks :, :] = ids.astype(jnp.bfloat16)
    copies[0].wait()
    for p in range(params):
        rows_ref[p] = jnp.where(inside, gradient_ref[p, 0], 0.0)
    copies[1].wait()
    for b in range(blocks):
        masked = rows_ref[:, b, :].astype(jnp.bfloat16)
        rows_ref[:, b, :] = jnp.dot(masked, basis_ref[0, b], preferred_element_type=jnp.float32)
    for p in range(params):
        payload_ref[p * blocks : (p + 1) * blocks, :] = rows_ref[p].astype(jnp.bfloat16)


def patch_sums(wanted, all_ref, params, blocks):
    members, _, width = all_ref.shape
    group = 128 // blocks
    tile = 4 * group
    total = jnp.zeros((wanted.shape[0], params * width), jnp.float32)
    for start in range(0, members, tile):
        ids = []
        for half in range(start, start + tile, group):
            ids.append(
                sum(all_ref[m, params * blocks :, :].astype(jnp.float32) for m in range(half, half + group))
            )
        ids = jnp.concatenate(ids, axis=1)
        patch = (ids[0:1] * PD + ids[1:2]).astype(jnp.int32)
        hit = jnp.where(wanted == patch, 1.0, 0.0).astype(jnp.bfloat16)
        values = jnp.concatenate(
            [
                jnp.concatenate(
                    [all_ref[m, p * blocks : (p + 1) * blocks, :] for m in range(start, start + tile)],
                    axis=0,
                )
                for p in range(params)
            ],
            axis=1,
        )
        total += jnp.dot(hit, values, preferred_element_type=jnp.float32)
    return total


def same_core():
    core = lax.axis_index("cuts") % CORES
    return [CORES * i + core for i in range(NEAR)]


def sums_kernel(
    offsets_ref, band_ref, radial_ref, wants_ref, all_ref, row_ref, basis_ref, out_ref, turned_ref
):
    for b in range(turned_ref.shape[0]):
        turned_ref[b] = basis_ref[0, b].T
    width = all_ref.shape[2]
    params, bands = band_ref.shape
    near, blocks, _ = out_ref.shape
    count = NEAR * blocks
    patches = all_ref.shape[0] * NEAR * PD
    wanted = jnp.concatenate([column(wants_ref[i : i + 1, :], blocks) for i in range(near)], axis=0)
    beside = patch_sums(wanted, row_ref, params, blocks)
    for p in range(params):
        lanes = slice(p * width, (p + 1) * width)
        radial = beside[:, lanes] * radial_ref[p]
        for i in range(near):
            out_ref[i, :, lanes] = radial[i * blocks : (i + 1) * blocks].astype(out_ref.dtype)
    mine = jnp.concatenate([column(wants_ref[pl.ds(i, 1), :], blocks) for i in same_core()], axis=0)
    wanted = [mine]
    for j in range(bands):
        moved = mine + offsets_ref[j]
        moved = jnp.where(moved < 0, moved + patches, moved)
        wanted.append(jnp.where(moved >= patches, moved - patches, moved))
    total = patch_sums(jnp.concatenate(wanted, axis=0), all_ref, params, blocks)
    core = lax.axis_index("cuts") % CORES
    for p in range(params):
        lanes = slice(p * width, (p + 1) * width)
        part = total[:, lanes]
        centre = part[:count]
        smooth = centre - (2.0 * radial_ref[p]) * centre
        for j in range(bands):
            shifted = part[(j + 1) * count : (j + 2) * count]
            smooth = smooth + band_ref[p, j] * (shifted - centre)
        radial = beside[:, lanes] * radial_ref[p]
        for i in range(NEAR):
            both = [radial[(CORES * i + c) * blocks : (CORES * i + c + 1) * blocks] for c in range(CORES)]
            added = jnp.where(core == 0, both[0], both[1]) + smooth[i * blocks : (i + 1) * blocks]
            out_ref[pl.ds(CORES * i + core, 1), :, lanes] = added[None].astype(out_ref.dtype)


def expand_kernel(parts_ref, turned_ref, valid_ref, out_ref, rows_ref):
    params, _, blocks, points = out_ref.shape
    width = turned_ref.shape[1]
    smooth = sum(parts_ref[i].astype(jnp.float32) for i in range(parts_ref.shape[0]))
    for p in range(params):
        rows_ref[p] = smooth[:, p * width : (p + 1) * width]
    for b in range(blocks):
        picked = rows_ref[:, b, :].astype(jnp.bfloat16)
        rows_ref[:, b, :] = jnp.dot(picked, turned_ref[b], preferred_element_type=jnp.float32)
    inside = inside_mask(valid_ref, blocks, points)
    for p in range(params):
        out_ref[p, 0] = jnp.where(inside, rows_ref[p], 0.0)


VMEM = pl.BlockSpec(memory_space=pltpu.VMEM)
HBM = pl.BlockSpec(memory_space=pltpu.HBM)
SMEM = pl.BlockSpec(memory_space=pltpu.SMEM)


def call(kernel, ins, out_shape, flops, scratch=()):
    many = isinstance(out_shape, tuple)
    return pl.pallas_call(
        kernel,
        out_shape=out_shape,
        in_specs=list(ins),
        out_specs=(VMEM,) * len(out_shape) if many else VMEM,
        scratch_shapes=list(scratch),
        compiler_params=pltpu.CompilerParams(vmem_limit_bytes=24 * 2**20),
        cost_estimate=pl.CostEstimate(flops=flops, bytes_accessed=2**21, transcendentals=0),
    )


def body(
    gradient, basis, block_owner, block_local, valid_count, band_offsets, band_weight, radial_weight
):
    params, _, blocks, points = gradient.shape
    width = basis.shape[3]
    cuts, rows = lax.axis_size("cuts"), lax.axis_size("group")
    chips = cuts // CORES
    values = params * width
    near = NEAR * CORES
    sets = [list(range(first, first + near)) for first in range(0, cuts, near)]
    own = block_owner[:, :, 0] * PD + block_local
    payload = call(
        project_kernel,
        [HBM] * 2 + [VMEM] * 2,
        jax.ShapeDtypeStruct((params * blocks + ID_ROWS, width), jnp.bfloat16),
        2 * blocks * params * points * width,
        [
            pltpu.VMEM(gradient.shape, gradient.dtype),
            pltpu.VMEM(basis.shape, basis.dtype),
            pltpu.VMEM((params, blocks, width), jnp.float32),
            pltpu.VMEM((ID_ROWS, 128), jnp.int32),
            pltpu.SemaphoreType.DMA((2,)),
        ],
    )(gradient, basis, own, valid_count)
    shares = [
        [CORES * z + c for z in range(first, chips, NEAR) for c in range(CORES)] for first in range(NEAR)
    ]
    gathered = lax.all_gather(payload, "cuts", axis_index_groups=shares)
    pairs = [
        (r * cuts + d, q * cuts + d)
        for r in range(rows)
        for d in range(cuts)
        for q in [r + 1 if d % CORES else r - 1]
        if 0 <= q < rows
    ]
    neighbour = lax.ppermute(gathered, ("group", "cuts"), pairs)
    position = lax.axis_index("cuts")
    member, lane = position // (NEAR * CORES) * CORES, position // (NEAR * CORES) % 2 * CORES
    ids = [
        lax.dynamic_slice(
            gathered, (member + c, params * blocks, (lane + c) * blocks), (1, 2, blocks)
        )[0].astype(jnp.int32)
        for c in range(CORES)
    ]
    ids = jnp.concatenate([each[0:1] * PD + each[1:2] for each in ids])
    lines = [[at + CORES * i + c for i in range(NEAR)] for at in range(0, cuts, near) for c in range(CORES)]
    wants = lax.all_gather(ids, "cuts", axis_index_groups=lines, tiled=True)
    one_hot = blocks * blocks * cuts * values
    for_near, turned = call(
        sums_kernel,
        [SMEM] * 3 + [VMEM] * 4,
        (
            jax.ShapeDtypeStruct((near, blocks, values), jnp.bfloat16),
            jax.ShapeDtypeStruct((blocks, width, points), basis.dtype),
        ),
        14 * one_hot,
    )(band_offsets, band_weight, radial_weight, wants, gathered, neighbour, basis)
    parts = lax.all_to_all(for_near, "cuts", 0, 0, axis_index_groups=sets, tiled=True)
    return call(
        expand_kernel,
        [VMEM] * 3,
        jax.ShapeDtypeStruct((params, 1, blocks, points), jnp.float32),
        2 * blocks * params * points * width,
        [pltpu.VMEM((params, blocks, width), jnp.float32)],
    )(parts, turned, valid_count)


def solution(mesh):
    return jax.shard_map(
        body,
        mesh=mesh,
        in_specs=(
            P(None, "group", "cuts", None),
            P("group", "cuts", None, None),
            P("group", "cuts", None),
            P("group", "cuts"),
            P("group", "cuts"),
            P(),
            P(),
            P(),
        ),
        out_specs=P(None, "group", "cuts", None),
        check_vma=False,
    )
```
